32 devices in a mesh: gx: 16 (over z, y, core), gy: 2 (over x).
Axes of the slice: x: 2, y: 2, z: 4, core: 2. Of those that a mesh axis runs over, the one named last changes fastest.
Arguments:
- source: float32 [64, 64, 256], P('gx', 'gy'), may hold values from -96 to 96
- region: int32 [64, 64, 256], P('gx', 'gy'), may hold values from 0 to 63
- permeability: float32 [64], replicated, may hold values from 0.1 to 10
- owners: int32 [16, 2], P('gx'), may hold values from 0 to 1
Outputs:
- pressure: float32 [64, 64, 256], P('gx', 'gy')
The draws below stay inside these ranges and needn't reach their ends.
All inputs are finite; a program needn't handle non-finite values.
Results may differ from the reference program's by a relative error of at most 0.0001.
Values sent between devices are 32-bit elements; how exact they have to be, the bound alone decides.
A program may use at most 64 MiB of HBM per device.

```python
import math
import jax
import jax.numpy as jnp

CX = 4
CY = 32
REGIONS = 64
PRE_SWEEPS = 2
POST_SWEEPS = 2
COARSE_SWEEPS = 6
NX = 64
NY = 64
NZ = 256
N_GX = 16
N_GY = 2


def with_ends(array, own_key, least, top_value):
    place = [jax.random.randint(jax.random.fold_in(own_key, axis), (), 0, length) for axis, length in enumerate(array.shape)]
    main_axis = array.shape.index(max(array.shape))
    next_to = place[:main_axis] + [(place[main_axis] + 1) % array.shape[main_axis]] + place[main_axis + 1:]
    return array.at[tuple(place)].set(least).at[tuple(next_to)].set(top_value)


def steps_of(rng, extent, pieces, low, largest):
    factor_of = 1.0
    for dim, blocks in pieces:
        draws = jax.random.uniform(jax.random.fold_in(jax.random.fold_in(rng, 6), dim), (blocks,), jnp.float32, low / len(pieces), largest / len(pieces))
        factor_of = factor_of * jnp.repeat(jnp.exp(draws), extent[dim] // blocks).reshape((-1,) + (1,) * (len(extent) - 1 - dim))
    return factor_of


def centred(own_key, dims, width, limit, shards=(), kind=jnp.bfloat16):
    loudness = steps_of(own_key, dims, shards, -0.22, 0.18) if shards else 1.0
    array = jax.random.normal(own_key, dims, jnp.float32) * width * loudness
    return jnp.minimum(jnp.maximum(array, -limit), limit).astype(kind)


def setup_inputs(seed: int = 0) -> dict:
    seeds = jax.random.split(jax.random.key(seed), 5)
    return {
        "source": centred(seeds[0], (NX, NY, NZ), 16.0, 96.0, ((0, 16), (1, 2)), jnp.float32),
        "region": with_ends(jax.random.randint(seeds[1], (NX, NY, NZ), 0, REGIONS), jax.random.fold_in(seeds[1], 1), 0, REGIONS - 1).astype(jnp.int32),
        "permeability": jnp.clip(jnp.exp(jax.random.uniform(seeds[2], (REGIONS,), jnp.float32, math.log(0.1), math.log(10.0))), 0.1, 10.0),
        "owners": with_ends(jax.random.randint(seeds[3], (N_GX, N_GY), 0, N_GY), jax.random.fold_in(seeds[3], 1), 0, N_GY - 1).astype(jnp.int32),
    }


RELAX_WEIGHT = 0.6
MASS_TERM = 0.1


def stencil_sum(padded):
    blended = 0.5 * padded[:-2] + padded[1:-1] + 0.5 * padded[2:]
    blended = 0.5 * blended[:, :-2] + blended[:, 1:-1] + 0.5 * blended[:, 2:]
    blended = 0.5 * blended[:, :, :-2] + blended[:, :, 1:-1] + 0.5 * blended[:, :, 2:]
    return 2.0 * (blended - padded[1:-1, 1:-1, 1:-1])


def pad_all(values):
    return jnp.pad(values, 1)


def operate(values, conduct, cond_pad, diagonal, factor, extend):
    value_pad = extend(values)
    return diagonal * values - factor * (conduct * stencil_sum(value_pad) + stencil_sum(cond_pad * value_pad))


def coarsen(values):
    size_x, size_y, size_z = values.shape
    return values.reshape(size_x // 2, 2, size_y // 2, 2, size_z // 2, 2).mean(axis=(1, 3, 5))


def local_ratio(numer, denom):
    return jnp.sum(numer) / jnp.maximum(jnp.sum(denom), 1.0)


def coarse_sweeps(residual, conduct, cond_pad, region_mask, extend, totals):
    diagonal = MASS_TERM + 0.125 * (14.0 * conduct + stencil_sum(cond_pad))
    correction = jnp.zeros_like(residual)
    for iteration in range(COARSE_SWEEPS):
        applied = operate(correction, conduct, cond_pad, diagonal, 0.125, extend)
        correction = region_mask * (correction + RELAX_WEIGHT * (residual - applied) / diagonal)
    applied = operate(correction, conduct, cond_pad, diagonal, 0.125, extend)
    ratio = totals(region_mask * (residual - applied), region_mask * diagonal)
    return correction + region_mask * ratio


def solve_region(residual, conduct, region_mask):
    return coarse_sweeps(residual, conduct, jnp.pad(conduct, 1), region_mask, pad_all, local_ratio)


def reference(source, region, permeability, owners):
    conduct = permeability[region]
    cond_pad = jnp.pad(conduct, 1)
    diagonal = MASS_TERM + 0.5 * (14.0 * conduct + stencil_sum(cond_pad))
    pressure = jnp.zeros_like(source)
    for iteration in range(PRE_SWEEPS):
        applied = operate(pressure, conduct, cond_pad, diagonal, 0.5, pad_all)
        pressure = pressure + RELAX_WEIGHT * (source - applied) / diagonal
    residual = source - operate(pressure, conduct, cond_pad, diagonal, 0.5, pad_all)
    coarse_res = coarsen(residual)
    coarse_cond = coarsen(conduct)
    size_x, size_y, size_z = coarse_res.shape
    slab_res = coarse_res.reshape(N_GX, CX // 2, size_y, size_z)
    slab_cond = coarse_cond.reshape(N_GX, CX // 2, size_y, size_z)
    owner_cells = jnp.repeat(owners, CY // 2, axis=1)
    correction = jnp.zeros_like(slab_res)
    for member in range(N_GY):
        region_mask = (owner_cells == member).astype(jnp.float32)[:, None, :, None]
        full_mask = jnp.broadcast_to(region_mask, slab_res.shape)
        correction = correction + jax.vmap(solve_region)(slab_res * region_mask, slab_cond * region_mask, full_mask)
    correction = correction.reshape(size_x, size_y, size_z)
    fine_corr = jnp.broadcast_to(correction[:, None, :, None, :, None], (size_x, 2, size_y, 2, size_z, 2)).reshape(source.shape)
    pressure = pressure + fine_corr
    for iteration in range(POST_SWEEPS):
        applied = operate(pressure, conduct, cond_pad, diagonal, 0.5, pad_all)
        pressure = pressure + RELAX_WEIGHT * (source - applied) / diagonal
    return pressure
```

```python
import functools

import jax
import jax.numpy as jnp
from jax import lax
from jax.experimental import pallas as pl
from jax.experimental.pallas import tpu as pltpu
from jax.sharding import PartitionSpec as P

POST_SWEEPS = 2
COARSE_SWEEPS = 6
RELAX_WEIGHT = 0.6
MASS_TERM = 0.1

MESH = pl.DeviceIdType.MESH
WIDE = 3
HALF = 4
COND, SOURCE, ITERATE = 0, 1, 2
WIDTHS = (3, 2, 2)
STEPS = ((-1, 0), (1, 0), (0, -1), (0, 1), (-1, -1), (1, -1), (-1, 1), (1, 1))


def kernel(
    n_gx, n_gy,
    owners_ref, table_ref, source_ref, region_ref, out_ref,
    ext, after, before, labels, weight, diag2, group, squeezed, whole_corr, spread,
    send_sem, recv_sem, g_send, g_recv, in_sem,
):
    nx, ny, nz = out_ref.shape
    cx, cy, cz = nx // 2, ny // 2, nz // 2
    first, last = WIDE, WIDE + nx
    gx, gy = lax.axis_index("gx"), lax.axis_index("gy")

    def exists(dx, dy):
        x, y = gx + dx, gy + dy
        return (x >= 0) & (x < n_gx) & (y >= 0) & (y < n_gy)

    load_source = pltpu.make_async_copy(
        source_ref, ext.at[SOURCE, pl.ds(first, nx), pl.ds(0, ny)], in_sem.at[0]
    )
    load_region = pltpu.make_async_copy(region_ref, labels, in_sem.at[1])
    load_region.start()
    load_source.start()

    barrier = pltpu.get_barrier_semaphore()
    count = jnp.int32(0)
    for dx, dy in STEPS:
        near = exists(dx, dy)

        @pl.when(near)
        def _():
            pl.semaphore_signal(
                barrier, inc=1, device_id=(gx + dx, gy + dy), device_id_type=MESH
            )

        count = count + near.astype(jnp.int32)
    for off in range(2 - n_gy - 1, n_gy):
        if abs(off) >= 2:
            near = exists(0, off)

            @pl.when(near)
            def _():
                pl.semaphore_signal(
                    barrier, inc=1, device_id=(gx, gy + off), device_id_type=MESH
                )

            count = count + near.astype(jnp.int32)

    def planes_in(dx, w):
        return {0: (first, nx), -1: (last, w), 1: (first - w, w)}[dx]

    def planes_out(dx, w):
        return {0: (first, nx), -1: (first, w), 1: (last - w, w)}[dx]

    def landing(kind, dx, dy, w):
        start, size = planes_in(dx, w)
        if dy == 0:
            return ext.at[kind, pl.ds(start, size), pl.ds(0, ny)]
        return (after if dy < 0 else before).at[kind, pl.ds(start, size)]

    def remote(kind, which):
        dx, dy = STEPS[which]
        w = WIDTHS[kind]
        start, size = planes_out(dx, w)
        rows = {0: pl.ds(0, ny), -1: pl.ds(0, 8), 1: pl.ds(ny - 8, 8)}[dy]
        return pltpu.make_async_remote_copy(
            src_ref=ext.at[kind, pl.ds(start, size), rows],
            dst_ref=landing(kind, dx, dy, w),
            send_sem=send_sem.at[kind, which],
            recv_sem=recv_sem.at[kind, which],
            device_id=(gx + dx, gy + dy),
            device_id_type=MESH,
        )

    def send(kind):
        for which, (dx, dy) in enumerate(STEPS):
            @pl.when(exists(dx, dy))
            def _():
                remote(kind, which).start()

    def receive(kind):
        for which, (dx, dy) in enumerate(STEPS):
            @pl.when(exists(-dx, -dy))
            def _():
                remote(kind, which).wait_recv()

    def finish(kind):
        for which, (dx, dy) in enumerate(STEPS):
            @pl.when(exists(dx, dy))
            def _():
                remote(kind, which).wait_send()

    for dx, dy in STEPS:
        @pl.when(jnp.logical_not(exists(-dx, -dy)))
        def _():
            for kind in range(3):
                ref = landing(kind, dx, dy, WIDTHS[kind])
                ref[...] = jnp.zeros(ref.shape, jnp.float32)

    row8 = lax.broadcasted_iota(jnp.int32, (8, nz), 0)

    def join(kind):
        w = WIDTHS[kind]
        for i in range(first - w, last + w):
            ext[kind, i, pl.ds(ny, 8), :] = jnp.where(
                row8 < HALF, after[kind, i], before[kind, i]
            )

    load_region.wait()
    pair = jnp.concatenate([table_ref[...], table_ref[...]], axis=1)
    table = jnp.broadcast_to(pair, (8, 128))
    for i in range(nx):
        for r in range(0, ny, 8):
            for c in range(0, nz, 128):
                spot = labels[i, pl.ds(r, 8), pl.ds(c, 128)]
                ext[COND, first + i, pl.ds(r, 8), pl.ds(c, 128)] = jnp.take_along_axis(
                    table, spot, axis=1
                )

    pl.semaphore_wait(barrier, count)
    send(COND)
    load_source.wait()
    send(SOURCE)

    lane = lax.broadcasted_iota(jnp.int32, (1, nz), 1)
    z_low = jnp.where(lane == 0, 0.0, 0.5)
    z_high = jnp.where(lane == nz - 1, 0.0, 0.5)
    rows = ny + 8

    def blend(a, b, c):
        u = b + 0.5 * (a + c)
        u = u + 0.5 * (pltpu.roll(u, 1, 0) + pltpu.roll(u, rows - 1, 0))
        return u + z_low * pltpu.roll(u, 1, 1) + z_high * pltpu.roll(u, nz - 1, 1)

    lane128 = lax.broadcasted_iota(jnp.int32, (8, 128), 1)
    even = lax.rem(2 * lane128, jnp.int32(128))
    half_of = lane128 // 2

    def coarsen(pairs, kind):
        for i, pair_sum in enumerate(pairs):
            total = pair_sum + pltpu.roll(pair_sum, nz - 1, 1)
            for r in range(0, ny, 8):
                low = jnp.take_along_axis(total[r:r + 8, :128], even, axis=1)
                high = jnp.take_along_axis(total[r:r + 8, 128:], even, axis=1)
                squeezed[i, pl.ds(r, 8), :] = jnp.where(lane128 < 64, low, high)
            block = squeezed[i, pl.ds(0, cy, stride=2), :] + squeezed[i, pl.ds(1, cy, stride=2), :]
            group[kind, i, pl.ds(pl.multiple_of(gy * cy, 8), cy), :] = 0.125 * block

    def gather(kind, off):
        mine = group.at[kind, :, pl.ds(pl.multiple_of(gy * cy, 8), cy)]
        return pltpu.make_async_remote_copy(
            src_ref=mine,
            dst_ref=mine,
            send_sem=g_send.at[kind, off - 1],
            recv_sem=g_recv.at[kind, off - 1],
            device_id=(gx, lax.rem(gy + off, n_gy)),
            device_id_type=MESH,
        )

    def gather_in(kind, off):
        sender = lax.rem(gy + n_gy - off, n_gy)
        theirs = group.at[kind, :, pl.ds(pl.multiple_of(sender * cy, 8), cy)]
        return pltpu.make_async_remote_copy(
            src_ref=theirs,
            dst_ref=theirs,
            send_sem=g_send.at[kind, off - 1],
            recv_sem=g_recv.at[kind, off - 1],
            device_id=(gx, sender),
            device_id_type=MESH,
        )

    coarsen(
        [ext[COND, first + 2 * i, pl.ds(0, ny), :] + ext[COND, first + 2 * i + 1, pl.ds(0, ny), :]
         for i in range(cx)],
        0,
    )
    for off in range(1, n_gy):
        gather(0, off).start()

    receive(COND)
    join(COND)
    row = lax.broadcasted_iota(jnp.int32, (rows, 1), 0)
    y = gy * ny + jnp.where(row < ny + HALF, row, row - rows)
    in_y = jnp.where((y >= 0) & (y < n_gy * ny), RELAX_WEIGHT, 0.0)
    for i in range(first - 2, last + 2):
        cond = ext[COND, i]
        mixed = blend(ext[COND, i - 1], cond, ext[COND, i + 1])
        x = gx * nx + (i - first)
        in_x = jnp.where((x >= 0) & (x < n_gx * nx), 1.0, 0.0)
        weight[i] = (in_y * in_x) / (MASS_TERM + 6.0 * cond + mixed)
        diag2[i] = MASS_TERM + 8.0 * cond + mixed

    def defect(kind, i, values, flux):
        lhs = ext[COND, i] * blend(values[i - 1], values[i], values[i + 1])
        return ext[SOURCE, i] - diag2[i] * values[i] + lhs + blend(flux[i - 1], flux[i], flux[i + 1])

    receive(SOURCE)
    join(SOURCE)
    values, flux = {}, {}
    for i in range(first - 2, last + 2):
        values[i] = weight[i] * ext[SOURCE, i]
        flux[i] = ext[COND, i] * values[i]
    smooth = {}
    for i in range(first - 1, last + 1):
        smooth[i] = values[i] + weight[i] * defect(SOURCE, i, values, flux)
    flux = {i: ext[COND, i] * smooth[i] for i in smooth}
    pairs = []
    for i in range(cx):
        j = first + 2 * i
        pairs.append(
            defect(SOURCE, j, smooth, flux)[:ny] + defect(SOURCE, j + 1, smooth, flux)[:ny]
        )
    coarsen(pairs, 1)
    for off in range(1, n_gy):
        gather(1, off).start()
    for i in range(first, last):
        ext[ITERATE, i, pl.ds(0, ny), :] = smooth[i][:ny]

    all_y = n_gy * cy
    crow = lax.broadcasted_iota(jnp.int32, (all_y, cz), 0)
    clane = lax.broadcasted_iota(jnp.int32, (all_y, cz), 1)
    owner = jnp.full((all_y, cz), owners_ref[0, 0], jnp.int32)
    for c in range(1, n_gy):
        owner = jnp.where(crow >= c * cy, owners_ref[0, c], owner)
    mask = jnp.where(owner == owners_ref[0, gy], 1.0, 0.0)
    y_low = jnp.where(crow == 0, 0.0, 0.5)
    y_high = jnp.where(crow == all_y - 1, 0.0, 0.5)
    cz_low = jnp.where(clane == 0, 0.0, 0.5)
    cz_high = jnp.where(clane == cz - 1, 0.0, 0.5)

    def coarse_blend(planes):
        mixed = []
        for i, u in enumerate(planes):
            if i > 0:
                u = u + 0.5 * planes[i - 1]
            if i + 1 < cx:
                u = u + 0.5 * planes[i + 1]
            u = u + y_low * pltpu.roll(u, 1, 0) + y_high * pltpu.roll(u, all_y - 1, 0)
            mixed.append(u + cz_low * pltpu.roll(u, 1, 1) + cz_high * pltpu.roll(u, cz - 1, 1))
        return mixed

    for off in range(1, n_gy):
        gather_in(0, off).wait_recv()
    cond_c = [mask * group[0, i] for i in range(cx)]
    mixed = coarse_blend(cond_c)
    diag_c = [MASS_TERM + 1.5 * k + 0.25 * b for k, b in zip(cond_c, mixed)]
    weight_c = [RELAX_WEIGHT * mask / d for d in diag_c]
    diag_sum = jnp.sum(functools.reduce(jnp.add, [mask * d for d in diag_c]), keepdims=True)

    for off in range(1, n_gy):
        gather_in(1, off).wait_recv()
    res_c = [mask * group[1, i] for i in range(cx)]

    def coarse_defect(e):
        straight = coarse_blend(e)
        carried = coarse_blend([k * v for k, v in zip(cond_c, e)])
        return [
            res_c[i] - (diag_c[i] + 0.5 * cond_c[i]) * e[i]
            + 0.25 * (cond_c[i] * straight[i] + carried[i])
            for i in range(cx)
        ]

    e = [w * r for w, r in zip(weight_c, res_c)]
    for _ in range(COARSE_SWEEPS - 1):
        d = coarse_defect(e)
        e = [e[i] + weight_c[i] * d[i] for i in range(cx)]
    d = coarse_defect(e)
    left = jnp.sum(functools.reduce(jnp.add, [mask * v for v in d]), keepdims=True)
    ratio = left / jnp.maximum(diag_sum, 1.0)
    for i in range(cx):
        whole_corr[i] = e[i] + mask * ratio
        mine = whole_corr[i, pl.ds(pl.multiple_of(gy * cy, 8), cy), :]
        spread[i, pl.ds(0, cy, stride=2), :] = mine
        spread[i, pl.ds(1, cy, stride=2), :] = mine
    for i in range(cx):
        for r in range(0, ny, 8):
            tile = spread[i, pl.ds(r, 8), :]
            for part in range(2):
                wide = jnp.take_along_axis(tile, half_of + 64 * part, axis=1)
                for j in (first + 2 * i, first + 2 * i + 1):
                    at = (ITERATE, j, pl.ds(r, 8), pl.ds(128 * part, 128))
                    ext[at] = ext[at] + wide

    send(ITERATE)
    receive(ITERATE)
    join(ITERATE)
    values = {i: ext[ITERATE, i] for i in range(first - 2, last + 2)}
    for sweep in range(POST_SWEEPS):
        reach = POST_SWEEPS - 1 - sweep
        flux = {i: ext[COND, i] * values[i] for i in values}
        values = {
            i: values[i] + weight[i] * defect(ITERATE, i, values, flux)
            for i in range(first - reach, last + reach)
        }
    for i in range(nx):
        out_ref[i] = values[first + i][:ny]

    for kind in range(3):
        finish(kind)
    for kind in range(2):
        for off in range(1, n_gy):
            gather(kind, off).wait_send()


def on_device(source, region, permeability, owners, *, n_gx, n_gy):
    nx, ny, nz = source.shape
    planes = nx + 2 * WIDE
    f32 = jnp.float32
    return pl.pallas_call(
        functools.partial(kernel, n_gx, n_gy),
        out_shape=jax.ShapeDtypeStruct(source.shape, f32),
        in_specs=[
            pl.BlockSpec(memory_space=pltpu.SMEM),
            pl.BlockSpec(memory_space=pltpu.VMEM),
            pl.BlockSpec(memory_space=pl.ANY),
            pl.BlockSpec(memory_space=pl.ANY),
        ],
        out_specs=pl.BlockSpec(memory_space=pltpu.VMEM),
        scratch_shapes=[
            pltpu.VMEM((3, planes, ny + 8, nz), f32),
            pltpu.VMEM((3, planes, 8, nz), f32),
            pltpu.VMEM((3, planes, 8, nz), f32),
            pltpu.VMEM((nx, ny, nz), jnp.int32),
            pltpu.VMEM((planes, ny + 8, nz), f32),
            pltpu.VMEM((planes, ny + 8, nz), f32),
            pltpu.VMEM((2, nx // 2, n_gy * ny // 2, nz // 2), f32),
            pltpu.VMEM((nx // 2, ny, nz // 2), f32),
            pltpu.VMEM((nx // 2, n_gy * ny // 2, nz // 2), f32),
            pltpu.VMEM((nx // 2, ny, nz // 2), f32),
            pltpu.SemaphoreType.DMA((3, 8)),
            pltpu.SemaphoreType.DMA((3, 8)),
            pltpu.SemaphoreType.DMA((2, n_gy - 1)),
            pltpu.SemaphoreType.DMA((2, n_gy - 1)),
            pltpu.SemaphoreType.DMA((2,)),
        ],
        compiler_params=pltpu.CompilerParams(
            collective_id=0, has_side_effects=True, vmem_limit_bytes=16 * 1024 * 1024
        ),
    )(owners, permeability[None, :], source, region)


def solution(mesh):
    placed = (P("gx", "gy", None), P("gx", "gy", None), P(), P("gx", None))
    body = functools.partial(on_device, n_gx=mesh.shape["gx"], n_gy=mesh.shape["gy"])
    return jax.shard_map(
        body, mesh=mesh, in_specs=placed, out_specs=P("gx", "gy", None), check_vma=False
    )
```

```python
import functools

import jax
import jax.numpy as jnp
from jax import lax
from jax.experimental import pallas as pl
from jax.experimental.pallas import tpu as pltpu
from jax.sharding import PartitionSpec as P

POST_SWEEPS = 2
COARSE_SWEEPS = 6
RELAX_WEIGHT = 0.6
MASS_TERM = 0.1

MESH = pl.DeviceIdType.MESH
WIDE = 3
HALF = 4
COND, SOURCE, ITERATE = 0, 1, 2
WIDTHS = (3, 2, 2)
STEPS = ((-1, 0), (1, 0), (0, -1), (0, 1), (-1, -1), (1, -1), (-1, 1), (1, 1))


def kernel(
    n_gx, n_gy,
    owners_in, table_in, source_ref, region_ref, out_ref,
    owners_ref, table_ref, ext, after, before, labels, weight, diag2, result, group, squeezed, whole_corr, spread,
    send_sem, recv_sem, g_send, g_recv, in_sem, out_sem,
):
    nx, ny, nz = out_ref.shape
    cx, cy, cz = nx // 2, ny // 2, nz // 2
    first, last = WIDE, WIDE + nx
    gx, gy = lax.axis_index("gx"), lax.axis_index("gy")

    def exists(dx, dy):
        x, y = gx + dx, gy + dy
        return (x >= 0) & (x < n_gx) & (y >= 0) & (y < n_gy)

    load_source = pltpu.make_async_copy(
        source_ref, ext.at[SOURCE, pl.ds(first, nx), pl.ds(0, ny)], in_sem.at[0]
    )
    load_region = pltpu.make_async_copy(region_ref, labels, in_sem.at[1])
    load_table = pltpu.make_async_copy(table_in, table_ref, in_sem.at[2])
    load_owners = pltpu.make_async_copy(owners_in, owners_ref, in_sem.at[3])
    load_region.start()
    load_table.start()
    load_source.start()
    load_owners.start()

    barrier = pltpu.get_barrier_semaphore()
    count = jnp.int32(0)
    for dx, dy in STEPS:
        near = exists(dx, dy)

        @pl.when(near)
        def _():
            pl.semaphore_signal(
                barrier, inc=1, device_id=(gx + dx, gy + dy), device_id_type=MESH
            )

        count = count + near.astype(jnp.int32)
    for off in range(2 - n_gy - 1, n_gy):
        if abs(off) >= 2:
            near = exists(0, off)

            @pl.when(near)
            def _():
                pl.semaphore_signal(
                    barrier, inc=1, device_id=(gx, gy + off), device_id_type=MESH
                )

            count = count + near.astype(jnp.int32)

    def planes_in(dx, w):
        return {0: (first, nx), -1: (last, w), 1: (first - w, w)}[dx]

    def planes_out(dx, w):
        return {0: (first, nx), -1: (first, w), 1: (last - w, w)}[dx]

    def landing(kind, dx, dy, w):
        start, size = planes_in(dx, w)
        if dy == 0:
            return ext.at[kind, pl.ds(start, size), pl.ds(0, ny)]
        return (after if dy < 0 else before).at[kind, pl.ds(start, size)]

    def remote(kind, which):
        dx, dy = STEPS[which]
        w = WIDTHS[kind]
        start, size = planes_out(dx, w)
        rows = {0: pl.ds(0, ny), -1: pl.ds(0, 8), 1: pl.ds(ny - 8, 8)}[dy]
        return pltpu.make_async_remote_copy(
            src_ref=ext.at[kind, pl.ds(start, size), rows],
            dst_ref=landing(kind, dx, dy, w),
            send_sem=send_sem.at[kind, which],
            recv_sem=recv_sem.at[kind, which],
            device_id=(gx + dx, gy + dy),
            device_id_type=MESH,
        )

    def send(kind):
        for which, (dx, dy) in enumerate(STEPS):
            @pl.when(exists(dx, dy))
            def _():
                remote(kind, which).start()

    def receive(kind):
        for which, (dx, dy) in enumerate(STEPS):
            @pl.when(exists(-dx, -dy))
            def _():
                remote(kind, which).wait_recv()

    def finish(kind):
        for which, (dx, dy) in enumerate(STEPS):
            @pl.when(exists(dx, dy))
            def _():
                remote(kind, which).wait_send()

    for dx, dy in STEPS:
        @pl.when(jnp.logical_not(exists(-dx, -dy)))
        def _():
            for kind in range(3):
                ref = landing(kind, dx, dy, WIDTHS[kind])
                ref[...] = jnp.zeros(ref.shape, jnp.float32)

    row8 = lax.broadcasted_iota(jnp.int32, (8, nz), 0)

    def join(kind):
        w = WIDTHS[kind]
        for i in range(first - w, last + w):
            ext[kind, i, pl.ds(ny, 8), :] = jnp.where(
                row8 < HALF, after[kind, i], before[kind, i]
            )

    load_table.wait()
    load_region.wait()
    pair = jnp.concatenate([table_ref[...], table_ref[...]], axis=1)
    table = jnp.broadcast_to(pair, (8, 128))
    for i in range(nx):
        for r in range(0, ny, 8):
            for c in range(0, nz, 128):
                spot = labels[i, pl.ds(r, 8), pl.ds(c, 128)]
                ext[COND, first + i, pl.ds(r, 8), pl.ds(c, 128)] = jnp.take_along_axis(
                    table, spot, axis=1
                )

    pl.semaphore_wait(barrier, count)
    send(COND)
    load_source.wait()
    send(SOURCE)
    load_owners.wait()

    lane = lax.broadcasted_iota(jnp.int32, (1, nz), 1)
    z_low = jnp.where(lane == 0, 0.0, 0.5)
    z_high = jnp.where(lane == nz - 1, 0.0, 0.5)
    rows = ny + 8

    def blend(a, b, c):
        u = b + 0.5 * (a + c)
        u = u + 0.5 * (pltpu.roll(u, 1, 0) + pltpu.roll(u, rows - 1, 0))
        return u + z_low * pltpu.roll(u, 1, 1) + z_high * pltpu.roll(u, nz - 1, 1)

    lane128 = lax.broadcasted_iota(jnp.int32, (8, 128), 1)
    even = lax.rem(2 * lane128, jnp.int32(128))
    half_of = lane128 // 2

    def coarsen(pairs, kind):
        for i, pair_sum in enumerate(pairs):
            total = pair_sum + pltpu.roll(pair_sum, nz - 1, 1)
            for r in range(0, ny, 8):
                low = jnp.take_along_axis(total[r:r + 8, :128], even, axis=1)
                high = jnp.take_along_axis(total[r:r + 8, 128:], even, axis=1)
                squeezed[i, pl.ds(r, 8), :] = jnp.where(lane128 < 64, low, high)
            block = squeezed[i, pl.ds(0, cy, stride=2), :] + squeezed[i, pl.ds(1, cy, stride=2), :]
            group[kind, i, pl.ds(pl.multiple_of(gy * cy, 8), cy), :] = 0.125 * block

    def gather(kind, off):
        mine = group.at[kind, :, pl.ds(pl.multiple_of(gy * cy, 8), cy)]
        return pltpu.make_async_remote_copy(
            src_ref=mine,
            dst_ref=mine,
            send_sem=g_send.at[kind, off - 1],
            recv_sem=g_recv.at[kind, off - 1],
            device_id=(gx, lax.rem(gy + off, n_gy)),
            device_id_type=MESH,
        )

    def gather_in(kind, off):
        sender = lax.rem(gy + n_gy - off, n_gy)
        theirs = group.at[kind, :, pl.ds(pl.multiple_of(sender * cy, 8), cy)]
        return pltpu.make_async_remote_copy(
            src_ref=theirs,
            dst_ref=theirs,
            send_sem=g_send.at[kind, off - 1],
            recv_sem=g_recv.at[kind, off - 1],
            device_id=(gx, sender),
            device_id_type=MESH,
        )

    coarsen(
        [ext[COND, first + 2 * i, pl.ds(0, ny), :] + ext[COND, first + 2 * i + 1, pl.ds(0, ny), :]
         for i in range(cx)],
        0,
    )
    for off in range(1, n_gy):
        gather(0, off).start()

    receive(COND)
    join(COND)
    row = lax.broadcasted_iota(jnp.int32, (rows, 1), 0)
    y = gy * ny + jnp.where(row < ny + HALF, row, row - rows)
    in_y = jnp.where((y >= 0) & (y < n_gy * ny), RELAX_WEIGHT, 0.0)
    for i in range(first - 2, last + 2):
        cond = ext[COND, i]
        mixed = blend(ext[COND, i - 1], cond, ext[COND, i + 1])
        x = gx * nx + (i - first)
        in_x = jnp.where((x >= 0) & (x < n_gx * nx), 1.0, 0.0)
        weight[i] = (in_y * in_x) / (MASS_TERM + 6.0 * cond + mixed)
        diag2[i] = MASS_TERM + 8.0 * cond + mixed

    def defect(kind, i, values, flux):
        lhs = ext[COND, i] * blend(values[i - 1], values[i], values[i + 1])
        return ext[SOURCE, i] - diag2[i] * values[i] + lhs + blend(flux[i - 1], flux[i], flux[i + 1])

    receive(SOURCE)
    join(SOURCE)
    values, flux = {}, {}
    for i in range(first - 2, last + 2):
        values[i] = weight[i] * ext[SOURCE, i]
        flux[i] = ext[COND, i] * values[i]
    smooth = {}
    for i in range(first - 1, last + 1):
        smooth[i] = values[i] + weight[i] * defect(SOURCE, i, values, flux)
    flux = {i: ext[COND, i] * smooth[i] for i in smooth}
    pairs = []
    for i in range(cx):
        j = first + 2 * i
        pairs.append(
            defect(SOURCE, j, smooth, flux)[:ny] + defect(SOURCE, j + 1, smooth, flux)[:ny]
        )
    coarsen(pairs, 1)
    for off in range(1, n_gy):
        gather(1, off).start()
    for i in range(first, last):
        ext[ITERATE, i, pl.ds(0, ny), :] = smooth[i][:ny]

    all_y = n_gy * cy
    crow = lax.broadcasted_iota(jnp.int32, (all_y, cz), 0)
    clane = lax.broadcasted_iota(jnp.int32, (all_y, cz), 1)
    owner = jnp.full((all_y, cz), owners_ref[0, 0], jnp.int32)
    for c in range(1, n_gy):
        owner = jnp.where(crow >= c * cy, owners_ref[0, c], owner)
    mask = jnp.where(owner == owners_ref[0, gy], 1.0, 0.0)
    y_low = jnp.where(crow == 0, 0.0, 0.5)
    y_high = jnp.where(crow == all_y - 1, 0.0, 0.5)
    cz_low = jnp.where(clane == 0, 0.0, 0.5)
    cz_high = jnp.where(clane == cz - 1, 0.0, 0.5)

    def coarse_blend(planes):
        mixed = []
        for i, u in enumerate(planes):
            if i > 0:
                u = u + 0.5 * planes[i - 1]
            if i + 1 < cx:
                u = u + 0.5 * planes[i + 1]
            u = u + y_low * pltpu.roll(u, 1, 0) + y_high * pltpu.roll(u, all_y - 1, 0)
            mixed.append(u + cz_low * pltpu.roll(u, 1, 1) + cz_high * pltpu.roll(u, cz - 1, 1))
        return mixed

    for off in range(1, n_gy):
        gather_in(0, off).wait_recv()
    cond_c = [mask * group[0, i] for i in range(cx)]
    mixed = coarse_blend(cond_c)
    diag_c = [MASS_TERM + 1.5 * k + 0.25 * b for k, b in zip(cond_c, mixed)]
    weight_c = [RELAX_WEIGHT * mask / d for d in diag_c]
    diag_sum = jnp.sum(functools.reduce(jnp.add, [mask * d for d in diag_c]), keepdims=True)

    for off in range(1, n_gy):
        gather_in(1, off).wait_recv()
    res_c = [mask * group[1, i] for i in range(cx)]

    def coarse_defect(e):
        straight = coarse_blend(e)
        carried = coarse_blend([k * v for k, v in zip(cond_c, e)])
        return [
            res_c[i] - (diag_c[i] + 0.5 * cond_c[i]) * e[i]
            + 0.25 * (cond_c[i] * straight[i] + carried[i])
            for i in range(cx)
        ]

    e = [w * r for w, r in zip(weight_c, res_c)]
    for _ in range(COARSE_SWEEPS - 1):
        d = coarse_defect(e)
        e = [e[i] + weight_c[i] * d[i] for i in range(cx)]
    d = coarse_defect(e)
    left = jnp.sum(functools.reduce(jnp.add, [mask * v for v in d]), keepdims=True)
    ratio = left / jnp.maximum(diag_sum, 1.0)
    for i in range(cx):
        whole_corr[i] = e[i] + mask * ratio
        mine = whole_corr[i, pl.ds(pl.multiple_of(gy * cy, 8), cy), :]
        spread[i, pl.ds(0, cy, stride=2), :] = mine
        spread[i, pl.ds(1, cy, stride=2), :] = mine
    for i in range(cx):
        for r in range(0, ny, 8):
            tile = spread[i, pl.ds(r, 8), :]
            for part in range(2):
                wide = jnp.take_along_axis(tile, half_of + 64 * part, axis=1)
                for j in (first + 2 * i, first + 2 * i + 1):
                    at = (ITERATE, j, pl.ds(r, 8), pl.ds(128 * part, 128))
                    ext[at] = ext[at] + wide

    send(ITERATE)
    receive(ITERATE)
    join(ITERATE)
    values = {i: ext[ITERATE, i] for i in range(first - 2, last + 2)}
    for sweep in range(POST_SWEEPS):
        reach = POST_SWEEPS - 1 - sweep
        flux = {i: ext[COND, i] * values[i] for i in values}
        values = {
            i: values[i] + weight[i] * defect(ITERATE, i, values, flux)
            for i in range(first - reach, last + reach)
        }
    stores = []
    for i in range(nx):
        result[i] = values[first + i][:ny]
        stores.append(pltpu.make_async_copy(result.at[i], out_ref.at[i], out_sem.at[i]))
        stores[i].start()

    for kind in range(3):
        finish(kind)
    for kind in range(2):
        for off in range(1, n_gy):
            gather(kind, off).wait_send()
    for store in stores:
        store.wait()


def on_device(source, region, permeability, owners, *, n_gx, n_gy):
    nx, ny, nz = source.shape
    planes = nx + 2 * WIDE
    f32 = jnp.float32
    return pl.pallas_call(
        functools.partial(kernel, n_gx, n_gy),
        out_shape=jax.ShapeDtypeStruct(source.shape, f32),
        in_specs=[
            pl.BlockSpec(memory_space=pltpu.HBM),
            pl.BlockSpec(memory_space=pltpu.HBM),
            pl.BlockSpec(memory_space=pltpu.HBM),
            pl.BlockSpec(memory_space=pltpu.HBM),
        ],
        out_specs=pl.BlockSpec(memory_space=pltpu.HBM),
        scratch_shapes=[
            pltpu.SMEM((1, n_gy), jnp.int32),
            pltpu.VMEM((1, permeability.shape[0]), f32),
            pltpu.VMEM((3, planes, ny + 8, nz), f32),
            pltpu.VMEM((3, planes, 8, nz), f32),
            pltpu.VMEM((3, planes, 8, nz), f32),
            pltpu.VMEM((nx, ny, nz), jnp.int32),
            pltpu.VMEM((planes, ny + 8, nz), f32),
            pltpu.VMEM((planes, ny + 8, nz), f32),
            pltpu.VMEM((nx, ny, nz), f32),
            pltpu.VMEM((2, nx // 2, n_gy * ny // 2, nz // 2), f32),
            pltpu.VMEM((nx // 2, ny, nz // 2), f32),
            pltpu.VMEM((nx // 2, n_gy * ny // 2, nz // 2), f32),
            pltpu.VMEM((nx // 2, ny, nz // 2), f32),
            pltpu.SemaphoreType.DMA((3, 8)),
            pltpu.SemaphoreType.DMA((3, 8)),
            pltpu.SemaphoreType.DMA((2, n_gy - 1)),
            pltpu.SemaphoreType.DMA((2, n_gy - 1)),
            pltpu.SemaphoreType.DMA((4,)),
            pltpu.SemaphoreType.DMA((nx,)),
        ],
        compiler_params=pltpu.CompilerParams(
            collective_id=0, has_side_effects=True, vmem_limit_bytes=60 * 1024 * 1024
        ),
    )(owners, permeability[None, :], source, region)


def solution(mesh):
    placed = (P("gx", "gy", None), P("gx", "gy", None), P(), P("gx", None))
    body = functools.partial(on_device, n_gx=mesh.shape["gx"], n_gy=mesh.shape["gy"])
    return jax.shard_map(
        body, mesh=mesh, in_specs=placed, out_specs=P("gx", "gy", None), check_vma=False
    )
```

```python
import functools

import jax
import jax.numpy as jnp
from jax import lax
from jax.experimental import pallas as pl
from jax.experimental.pallas import tpu as pltpu
from jax.sharding import PartitionSpec as P

POST_SWEEPS = 2
COARSE_SWEEPS = 6
RELAX_WEIGHT = 0.6
MASS_TERM = 0.1

MESH = pl.DeviceIdType.MESH
WIDE = 3
HALF = 4
COND, SOURCE, ITERATE = 0, 1, 2
WIDTHS = (3, 2, 2)
STEPS = ((-1, 0), (1, 0), (0, -1), (0, 1), (-1, -1), (1, -1), (-1, 1), (1, 1))


def kernel(
    n_gx, n_gy,
    owners_in, table_in, source_ref, region_ref, out_ref,
    owners_ref, table_ref, ext, packed, after, before, labels, weight, diag2, result, group, squeezed, whole_corr, spread,
    send_sem, recv_sem, g_send, g_recv, in_sem, out_sem,
):
    nx, ny, nz = out_ref.shape
    cx, cy, cz = nx // 2, ny // 2, nz // 2
    first, last = WIDE, WIDE + nx
    gx, gy = lax.axis_index("gx"), lax.axis_index("gy")

    def exists(dx, dy):
        x, y = gx + dx, gy + dy
        return (x >= 0) & (x < n_gx) & (y >= 0) & (y < n_gy)

    load_source = pltpu.make_async_copy(
        source_ref, ext.at[SOURCE, pl.ds(first, nx), pl.ds(0, ny)], in_sem.at[0]
    )
    load_region = pltpu.make_async_copy(region_ref, labels, in_sem.at[1])
    load_table = pltpu.make_async_copy(table_in, table_ref, in_sem.at[2])
    load_owners = pltpu.make_async_copy(owners_in, owners_ref, in_sem.at[3])
    load_region.start()
    load_table.start()
    load_source.start()
    load_owners.start()

    barrier = pltpu.get_barrier_semaphore()
    count = jnp.int32(0)
    for dx, dy in STEPS:
        near = exists(dx, dy)

        @pl.when(near)
        def _():
            pl.semaphore_signal(
                barrier, inc=1, device_id=(gx + dx, gy + dy), device_id_type=MESH
            )

        count = count + near.astype(jnp.int32)
    for off in range(2 - n_gy - 1, n_gy):
        if abs(off) >= 2:
            near = exists(0, off)

            @pl.when(near)
            def _():
                pl.semaphore_signal(
                    barrier, inc=1, device_id=(gx, gy + off), device_id_type=MESH
                )

            count = count + near.astype(jnp.int32)

    def planes_in(dx, w):
        return {0: (first, nx), -1: (last, w), 1: (first - w, w)}[dx]

    def planes_out(dx, w):
        return {0: (first, nx), -1: (first, w), 1: (last - w, w)}[dx]

    def landing(kind, dx, dy, w):
        start, size = planes_in(dx, w)
        if dy == 0:
            return ext.at[kind, pl.ds(start, size), pl.ds(0, ny)]
        start, size = {0: (2, cx), -1: (2 + cx, (w + 1) // 2), 1: (2 - (w + 1) // 2, (w + 1) // 2)}[dx]
        return (after if dy < 0 else before).at[kind, pl.ds(start, size)]

    def remote(kind, which):
        dx, dy = STEPS[which]
        w = WIDTHS[kind]
        start, size = planes_out(dx, w)
        if dy == 0:
            source = ext.at[kind, pl.ds(start, size), pl.ds(0, ny)]
        else:
            tiles = (w + 1) // 2
            start, size = {0: (0, cx), -1: (0, tiles), 1: (cx - tiles, tiles)}[dx]
            source = packed.at[kind, max(dy, 0), pl.ds(start, size)]
        return pltpu.make_async_remote_copy(
            src_ref=source,
            dst_ref=landing(kind, dx, dy, w),
            send_sem=send_sem.at[kind, which],
            recv_sem=recv_sem.at[kind, which],
            device_id=(gx + dx, gy + dy),
            device_id_type=MESH,
        )

    def send(kind):
        for which, (dx, dy) in enumerate(STEPS):
            @pl.when(exists(dx, dy))
            def _():
                remote(kind, which).start()

    def receive(kind):
        for which, (dx, dy) in enumerate(STEPS):
            @pl.when(exists(-dx, -dy))
            def _():
                remote(kind, which).wait_recv()

    def finish(kind):
        for which, (dx, dy) in enumerate(STEPS):
            @pl.when(exists(dx, dy))
            def _():
                remote(kind, which).wait_send()

    for dx, dy in STEPS:
        @pl.when(jnp.logical_not(exists(-dx, -dy)))
        def _():
            for kind in range(3):
                ref = landing(kind, dx, dy, WIDTHS[kind])
                ref[...] = jnp.zeros(ref.shape, jnp.float32)

    row8 = lax.broadcasted_iota(jnp.int32, (8, nz), 0)

    def pack(kind):
        for s in range(cx):
            a, b = first + 2 * s, first + 2 * s + 1
            packed[kind, 0, s] = jnp.where(
                row8 < HALF, ext[kind, a, pl.ds(0, 8), :],
                pltpu.roll(ext[kind, b, pl.ds(0, 8), :], HALF, 0),
            )
            packed[kind, 1, s] = jnp.where(
                row8 < HALF, pltpu.roll(ext[kind, a, pl.ds(ny - 8, 8), :], HALF, 0),
                ext[kind, b, pl.ds(ny - 8, 8), :],
            )

    def join(kind):
        w = WIDTHS[kind]
        for i in range(first - w, last + w):
            s, odd = divmod(i - first + 4, 2)
            low, high = after[kind, s], before[kind, s]
            if odd:
                low = pltpu.roll(low, HALF, 0)
            else:
                high = pltpu.roll(high, HALF, 0)
            ext[kind, i, pl.ds(ny, 8), :] = jnp.where(row8 < HALF, low, high)

    load_table.wait()
    load_region.wait()
    pair = jnp.concatenate([table_ref[...], table_ref[...]], axis=1)
    table = jnp.broadcast_to(pair, (8, 128))
    for i in range(nx):
        for r in range(0, ny, 8):
            for c in range(0, nz, 128):
                spot = labels[i, pl.ds(r, 8), pl.ds(c, 128)]
                ext[COND, first + i, pl.ds(r, 8), pl.ds(c, 128)] = jnp.take_along_axis(
                    table, spot, axis=1
                )

    pack(COND)
    pl.semaphore_wait(barrier, count)
    send(COND)
    load_source.wait()
    pack(SOURCE)
    send(SOURCE)
    load_owners.wait()

    lane = lax.broadcasted_iota(jnp.int32, (1, nz), 1)
    z_low = jnp.where(lane == 0, 0.0, 0.5)
    z_high = jnp.where(lane == nz - 1, 0.0, 0.5)
    rows = ny + 8

    def blend(a, b, c):
        u = b + 0.5 * (a + c)
        u = u + 0.5 * (pltpu.roll(u, 1, 0) + pltpu.roll(u, rows - 1, 0))
        return u + z_low * pltpu.roll(u, 1, 1) + z_high * pltpu.roll(u, nz - 1, 1)

    lane128 = lax.broadcasted_iota(jnp.int32, (8, 128), 1)
    even = lax.rem(2 * lane128, jnp.int32(128))
    half_of = lane128 // 2

    def coarsen(pairs, kind):
        for i, pair_sum in enumerate(pairs):
            total = pair_sum + pltpu.roll(pair_sum, nz - 1, 1)
            for r in range(0, ny, 8):
                low = jnp.take_along_axis(total[r:r + 8, :128], even, axis=1)
                high = jnp.take_along_axis(total[r:r + 8, 128:], even, axis=1)
                squeezed[i, pl.ds(r, 8), :] = jnp.where(lane128 < 64, low, high)
            block = squeezed[i, pl.ds(0, cy, stride=2), :] + squeezed[i, pl.ds(1, cy, stride=2), :]
            group[kind, i, pl.ds(pl.multiple_of(gy * cy, 8), cy), :] = 0.125 * block

    def gather(kind, off):
        mine = group.at[kind, :, pl.ds(pl.multiple_of(gy * cy, 8), cy)]
        return pltpu.make_async_remote_copy(
            src_ref=mine,
            dst_ref=mine,
            send_sem=g_send.at[kind, off - 1],
            recv_sem=g_recv.at[kind, off - 1],
            device_id=(gx, lax.rem(gy + off, n_gy)),
            device_id_type=MESH,
        )

    def gather_in(kind, off):
        sender = lax.rem(gy + n_gy - off, n_gy)
        theirs = group.at[kind, :, pl.ds(pl.multiple_of(sender * cy, 8), cy)]
        return pltpu.make_async_remote_copy(
            src_ref=theirs,
            dst_ref=theirs,
            send_sem=g_send.at[kind, off - 1],
            recv_sem=g_recv.at[kind, off - 1],
            device_id=(gx, sender),
            device_id_type=MESH,
        )

    coarsen(
        [ext[COND, first + 2 * i, pl.ds(0, ny), :] + ext[COND, first + 2 * i + 1, pl.ds(0, ny), :]
         for i in range(cx)],
        0,
    )
    for off in range(1, n_gy):
        gather(0, off).start()

    receive(COND)
    join(COND)
    row = lax.broadcasted_iota(jnp.int32, (rows, 1), 0)
    y = gy * ny + jnp.where(row < ny + HALF, row, row - rows)
    in_y = jnp.where((y >= 0) & (y < n_gy * ny), RELAX_WEIGHT, 0.0)
    for i in range(first - 2, last + 2):
        cond = ext[COND, i]
        mixed = blend(ext[COND, i - 1], cond, ext[COND, i + 1])
        x = gx * nx + (i - first)
        in_x = jnp.where((x >= 0) & (x < n_gx * nx), 1.0, 0.0)
        weight[i] = (in_y * in_x) / (MASS_TERM + 6.0 * cond + mixed)
        diag2[i] = MASS_TERM + 8.0 * cond + mixed

    def defect(kind, i, values, flux):
        lhs = ext[COND, i] * blend(values[i - 1], values[i], values[i + 1])
        return ext[SOURCE, i] - diag2[i] * values[i] + lhs + blend(flux[i - 1], flux[i], flux[i + 1])

    receive(SOURCE)
    join(SOURCE)
    values, flux = {}, {}
    for i in range(first - 2, last + 2):
        values[i] = weight[i] * ext[SOURCE, i]
        flux[i] = ext[COND, i] * values[i]
    smooth = {}
    for i in range(first - 1, last + 1):
        smooth[i] = values[i] + weight[i] * defect(SOURCE, i, values, flux)
    flux = {i: ext[COND, i] * smooth[i] for i in smooth}
    pairs = []
    for i in range(cx):
        j = first + 2 * i
        pairs.append(
            defect(SOURCE, j, smooth, flux)[:ny] + defect(SOURCE, j + 1, smooth, flux)[:ny]
        )
    coarsen(pairs, 1)
    for off in range(1, n_gy):
        gather(1, off).start()
    for i in range(first, last):
        ext[ITERATE, i, pl.ds(0, ny), :] = smooth[i][:ny]

    all_y = n_gy * cy
    crow = lax.broadcasted_iota(jnp.int32, (all_y, cz), 0)
    clane = lax.broadcasted_iota(jnp.int32, (all_y, cz), 1)
    owner = jnp.full((all_y, cz), owners_ref[0, 0], jnp.int32)
    for c in range(1, n_gy):
        owner = jnp.where(crow >= c * cy, owners_ref[0, c], owner)
    mask = jnp.where(owner == owners_ref[0, gy], 1.0, 0.0)
    y_low = jnp.where(crow == 0, 0.0, 0.5)
    y_high = jnp.where(crow == all_y - 1, 0.0, 0.5)
    cz_low = jnp.where(clane == 0, 0.0, 0.5)
    cz_high = jnp.where(clane == cz - 1, 0.0, 0.5)

    def coarse_blend(planes):
        mixed = []
        for i, u in enumerate(planes):
            if i > 0:
                u = u + 0.5 * planes[i - 1]
            if i + 1 < cx:
                u = u + 0.5 * planes[i + 1]
            u = u + y_low * pltpu.roll(u, 1, 0) + y_high * pltpu.roll(u, all_y - 1, 0)
            mixed.append(u + cz_low * pltpu.roll(u, 1, 1) + cz_high * pltpu.roll(u, cz - 1, 1))
        return mixed

    for off in range(1, n_gy):
        gather_in(0, off).wait_recv()
    cond_c = [mask * group[0, i] for i in range(cx)]
    mixed = coarse_blend(cond_c)
    diag_c = [MASS_TERM + 1.5 * k + 0.25 * b for k, b in zip(cond_c, mixed)]
    weight_c = [RELAX_WEIGHT * mask / d for d in diag_c]
    diag_sum = jnp.sum(functools.reduce(jnp.add, [mask * d for d in diag_c]), keepdims=True)

    for off in range(1, n_gy):
        gather_in(1, off).wait_recv()
    res_c = [mask * group[1, i] for i in range(cx)]

    def coarse_defect(e):
        straight = coarse_blend(e)
        carried = coarse_blend([k * v for k, v in zip(cond_c, e)])
        return [
            res_c[i] - (diag_c[i] + 0.5 * cond_c[i]) * e[i]
            + 0.25 * (cond_c[i] * straight[i] + carried[i])
            for i in range(cx)
        ]

    e = [w * r for w, r in zip(weight_c, res_c)]
    for _ in range(COARSE_SWEEPS - 1):
        d = coarse_defect(e)
        e = [e[i] + weight_c[i] * d[i] for i in range(cx)]
    d = coarse_defect(e)
    left = jnp.sum(functools.reduce(jnp.add, [mask * v for v in d]), keepdims=True)
    ratio = left / jnp.maximum(diag_sum, 1.0)
    for i in range(cx):
        whole_corr[i] = e[i] + mask * ratio
        mine = whole_corr[i, pl.ds(pl.multiple_of(gy * cy, 8), cy), :]
        spread[i, pl.ds(0, cy, stride=2), :] = mine
        spread[i, pl.ds(1, cy, stride=2), :] = mine
    for i in range(cx):
        for r in range(0, ny, 8):
            tile = spread[i, pl.ds(r, 8), :]
            for part in range(2):
                wide = jnp.take_along_axis(tile, half_of + 64 * part, axis=1)
                for j in (first + 2 * i, first + 2 * i + 1):
                    at = (ITERATE, j, pl.ds(r, 8), pl.ds(128 * part, 128))
                    ext[at] = ext[at] + wide

    pack(ITERATE)
    send(ITERATE)
    receive(ITERATE)
    join(ITERATE)
    values = {i: ext[ITERATE, i] for i in range(first - 2, last + 2)}
    for sweep in range(POST_SWEEPS):
        reach = POST_SWEEPS - 1 - sweep
        flux = {i: ext[COND, i] * values[i] for i in values}
        values = {
            i: values[i] + weight[i] * defect(ITERATE, i, values, flux)
            for i in range(first - reach, last + reach)
        }
    stores = []
    for i in range(nx):
        result[i] = values[first + i][:ny]
        stores.append(pltpu.make_async_copy(result.at[i], out_ref.at[i], out_sem.at[i]))
        stores[i].start()

    for kind in range(3):
        finish(kind)
    for kind in range(2):
        for off in range(1, n_gy):
            gather(kind, off).wait_send()
    for store in stores:
        store.wait()


def on_device(source, region, permeability, owners, *, n_gx, n_gy):
    nx, ny, nz = source.shape
    planes = nx + 2 * WIDE
    f32 = jnp.float32
    return pl.pallas_call(
        functools.partial(kernel, n_gx, n_gy),
        out_shape=jax.ShapeDtypeStruct(source.shape, f32),
        in_specs=[
            pl.BlockSpec(memory_space=pltpu.HBM),
            pl.BlockSpec(memory_space=pltpu.HBM),
            pl.BlockSpec(memory_space=pltpu.HBM),
            pl.BlockSpec(memory_space=pltpu.HBM),
        ],
        out_specs=pl.BlockSpec(memory_space=pltpu.HBM),
        scratch_shapes=[
            pltpu.SMEM((1, n_gy), jnp.int32),
            pltpu.VMEM((1, permeability.shape[0]), f32),
            pltpu.VMEM((3, planes, ny + 8, nz), f32),
            pltpu.VMEM((3, 2, nx // 2, 8, nz), f32),
            pltpu.VMEM((3, nx // 2 + 4, 8, nz), f32),
            pltpu.VMEM((3, nx // 2 + 4, 8, nz), f32),
            pltpu.VMEM((nx, ny, nz), jnp.int32),
            pltpu.VMEM((planes, ny + 8, nz), f32),
            pltpu.VMEM((planes, ny + 8, nz), f32),
            pltpu.VMEM((nx, ny, nz), f32),
            pltpu.VMEM((2, nx // 2, n_gy * ny // 2, nz // 2), f32),
            pltpu.VMEM((nx // 2, ny, nz // 2), f32),
            pltpu.VMEM((nx // 2, n_gy * ny // 2, nz // 2), f32),
            pltpu.VMEM((nx // 2, ny, nz // 2), f32),
            pltpu.SemaphoreType.DMA((3, 8)),
            pltpu.SemaphoreType.DMA((3, 8)),
            pltpu.SemaphoreType.DMA((2, n_gy - 1)),
            pltpu.SemaphoreType.DMA((2, n_gy - 1)),
            pltpu.SemaphoreType.DMA((4,)),
            pltpu.SemaphoreType.DMA((nx,)),
        ],
        compiler_params=pltpu.CompilerParams(
            collective_id=0, has_side_effects=True, vmem_limit_bytes=60 * 1024 * 1024
        ),
    )(owners, permeability[None, :], source, region)


def solution(mesh):
    placed = (P("gx", "gy", None), P("gx", "gy", None), P(), P("gx", None))
    body = functools.partial(on_device, n_gx=mesh.shape["gx"], n_gy=mesh.shape["gy"])
    return jax.shard_map(
        body, mesh=mesh, in_specs=placed, out_specs=P("gx", "gy", None), check_vma=False
    )
```

```python
import functools

import jax
import jax.numpy as jnp
from jax import lax
from jax.experimental import pallas as pl
from jax.experimental.pallas import tpu as pltpu
from jax.sharding import PartitionSpec as P

POST_SWEEPS = 2
COARSE_SWEEPS = 6
RELAX_WEIGHT = 0.6
MASS_TERM = 0.1

MESH = pl.DeviceIdType.MESH
WIDE = 3
HALF = 4
COND, SOURCE, ITERATE = 0, 1, 2
WIDTHS = (3, 2, 2)
STEPS = ((-1, 0), (1, 0), (0, -1), (0, 1), (-1, -1), (1, -1), (-1, 1), (1, 1))


def kernel(
    n_gx, n_gy,
    owners_in, table_in, source_ref, region_ref, out_ref,
    owners_ref, table_ref, ext, packed, after, before, labels, weight, diag2, result, group, squeezed, whole_corr, spread, corr, corr_y, wide,
    send_sem, recv_sem, g_send, g_recv, in_sem, out_sem, c_send, c_recv,
):
    nx, ny, nz = out_ref.shape
    cx, cy, cz = nx // 2, ny // 2, nz // 2
    first, last = WIDE, WIDE + nx
    gx, gy = lax.axis_index("gx"), lax.axis_index("gy")

    def exists(dx, dy):
        x, y = gx + dx, gy + dy
        return (x >= 0) & (x < n_gx) & (y >= 0) & (y < n_gy)

    load_source = pltpu.make_async_copy(
        source_ref, ext.at[SOURCE, pl.ds(first, nx), pl.ds(0, ny)], in_sem.at[0]
    )
    load_region = pltpu.make_async_copy(region_ref, labels, in_sem.at[1])
    load_table = pltpu.make_async_copy(table_in, table_ref, in_sem.at[2])
    load_owners = pltpu.make_async_copy(owners_in, owners_ref, in_sem.at[3])
    load_region.start()
    load_table.start()
    load_source.start()
    load_owners.start()

    barrier = pltpu.get_barrier_semaphore()
    count = jnp.int32(0)
    for dx, dy in STEPS:
        near = exists(dx, dy)

        @pl.when(near)
        def _():
            pl.semaphore_signal(
                barrier, inc=1, device_id=(gx + dx, gy + dy), device_id_type=MESH
            )

        count = count + near.astype(jnp.int32)
    for off in range(2 - n_gy - 1, n_gy):
        if abs(off) >= 2:
            near = exists(0, off)

            @pl.when(near)
            def _():
                pl.semaphore_signal(
                    barrier, inc=1, device_id=(gx, gy + off), device_id_type=MESH
                )

            count = count + near.astype(jnp.int32)

    def planes_in(dx, w):
        return {0: (first, nx), -1: (last, w), 1: (first - w, w)}[dx]

    def planes_out(dx, w):
        return {0: (first, nx), -1: (first, w), 1: (last - w, w)}[dx]

    def landing(kind, dx, dy, w):
        start, size = planes_in(dx, w)
        if dy == 0:
            return ext.at[kind, pl.ds(start, size), pl.ds(0, ny)]
        start, size = {0: (2, cx), -1: (2 + cx, (w + 1) // 2), 1: (2 - (w + 1) // 2, (w + 1) // 2)}[dx]
        return (after if dy < 0 else before).at[kind, pl.ds(start, size)]

    def remote(kind, which):
        dx, dy = STEPS[which]
        w = WIDTHS[kind]
        start, size = planes_out(dx, w)
        if dy == 0:
            source = ext.at[kind, pl.ds(start, size), pl.ds(0, ny)]
        else:
            tiles = (w + 1) // 2
            start, size = {0: (0, cx), -1: (0, tiles), 1: (cx - tiles, tiles)}[dx]
            source = packed.at[kind, max(dy, 0), pl.ds(start, size)]
        return pltpu.make_async_remote_copy(
            src_ref=source,
            dst_ref=landing(kind, dx, dy, w),
            send_sem=send_sem.at[kind, which],
            recv_sem=recv_sem.at[kind, which],
            device_id=(gx + dx, gy + dy),
            device_id_type=MESH,
        )

    def landing_corr(dx, dy):
        at = {0: pl.ds(1, cx), -1: pl.ds(cx + 1, 1), 1: pl.ds(0, 1)}[dx]
        return corr.at[at] if dy == 0 else corr_y.at[max(dy, 0), at]

    def remote_corr(which):
        dx, dy = STEPS[which]
        at = {0: pl.ds(1, cx), -1: pl.ds(1, 1), 1: pl.ds(cx, 1)}[dx]
        rows = {0: pl.ds(0, cy), -1: pl.ds(0, 8), 1: pl.ds(cy - 8, 8)}[dy]
        return pltpu.make_async_remote_copy(
            src_ref=corr.at[at, rows],
            dst_ref=landing_corr(dx, dy),
            send_sem=c_send.at[which],
            recv_sem=c_recv.at[which],
            device_id=(gx + dx, gy + dy),
            device_id_type=MESH,
        )

    def send(kind):
        for which, (dx, dy) in enumerate(STEPS):
            @pl.when(exists(dx, dy))
            def _():
                remote(kind, which).start()

    def receive(kind):
        for which, (dx, dy) in enumerate(STEPS):
            @pl.when(exists(-dx, -dy))
            def _():
                remote(kind, which).wait_recv()

    def finish(kind):
        for which, (dx, dy) in enumerate(STEPS):
            @pl.when(exists(dx, dy))
            def _():
                remote(kind, which).wait_send()

    for dx, dy in STEPS:
        @pl.when(jnp.logical_not(exists(-dx, -dy)))
        def _():
            for kind in range(3):
                ref = landing(kind, dx, dy, WIDTHS[kind])
                ref[...] = jnp.zeros(ref.shape, jnp.float32)
            ref = landing_corr(dx, dy)
            ref[...] = jnp.zeros(ref.shape, jnp.float32)

    row8 = lax.broadcasted_iota(jnp.int32, (8, nz), 0)

    def pack(kind):
        for s in range(cx):
            a, b = first + 2 * s, first + 2 * s + 1
            packed[kind, 0, s] = jnp.where(
                row8 < HALF, ext[kind, a, pl.ds(0, 8), :],
                pltpu.roll(ext[kind, b, pl.ds(0, 8), :], HALF, 0),
            )
            packed[kind, 1, s] = jnp.where(
                row8 < HALF, pltpu.roll(ext[kind, a, pl.ds(ny - 8, 8), :], HALF, 0),
                ext[kind, b, pl.ds(ny - 8, 8), :],
            )

    def join(kind):
        w = WIDTHS[kind]
        for i in range(first - w, last + w):
            s, odd = divmod(i - first + 4, 2)
            low, high = after[kind, s], before[kind, s]
            if odd:
                low = pltpu.roll(low, HALF, 0)
            else:
                high = pltpu.roll(high, HALF, 0)
            ext[kind, i, pl.ds(ny, 8), :] = jnp.where(row8 < HALF, low, high)

    load_table.wait()
    load_region.wait()
    pair = jnp.concatenate([table_ref[...], table_ref[...]], axis=1)
    table = jnp.broadcast_to(pair, (8, 128))
    for i in range(nx):
        for r in range(0, ny, 8):
            for c in range(0, nz, 128):
                spot = labels[i, pl.ds(r, 8), pl.ds(c, 128)]
                ext[COND, first + i, pl.ds(r, 8), pl.ds(c, 128)] = jnp.take_along_axis(
                    table, spot, axis=1
                )

    pack(COND)
    pl.semaphore_wait(barrier, count)
    send(COND)
    load_source.wait()
    pack(SOURCE)
    send(SOURCE)
    load_owners.wait()

    lane = lax.broadcasted_iota(jnp.int32, (1, nz), 1)
    z_low = jnp.where(lane == 0, 0.0, 0.5)
    z_high = jnp.where(lane == nz - 1, 0.0, 0.5)
    rows = ny + 8

    def blend(a, b, c):
        u = b + 0.5 * (a + c)
        u = u + 0.5 * (pltpu.roll(u, 1, 0) + pltpu.roll(u, rows - 1, 0))
        return u + z_low * pltpu.roll(u, 1, 1) + z_high * pltpu.roll(u, nz - 1, 1)

    lane128 = lax.broadcasted_iota(jnp.int32, (8, 128), 1)
    even = lax.rem(2 * lane128, jnp.int32(128))
    half_of = lane128 // 2

    def coarsen(pairs, kind):
        for i, pair_sum in enumerate(pairs):
            total = pair_sum + pltpu.roll(pair_sum, nz - 1, 1)
            for r in range(0, ny, 8):
                low = jnp.take_along_axis(total[r:r + 8, :128], even, axis=1)
                high = jnp.take_along_axis(total[r:r + 8, 128:], even, axis=1)
                squeezed[i, pl.ds(r, 8), :] = jnp.where(lane128 < 64, low, high)
            block = squeezed[i, pl.ds(0, cy, stride=2), :] + squeezed[i, pl.ds(1, cy, stride=2), :]
            group[kind, i, pl.ds(pl.multiple_of(gy * cy, 8), cy), :] = 0.125 * block

    def gather(kind, off):
        mine = group.at[kind, :, pl.ds(pl.multiple_of(gy * cy, 8), cy)]
        return pltpu.make_async_remote_copy(
            src_ref=mine,
            dst_ref=mine,
            send_sem=g_send.at[kind, off - 1],
            recv_sem=g_recv.at[kind, off - 1],
            device_id=(gx, lax.rem(gy + off, n_gy)),
            device_id_type=MESH,
        )

    def gather_in(kind, off):
        sender = lax.rem(gy + n_gy - off, n_gy)
        theirs = group.at[kind, :, pl.ds(pl.multiple_of(sender * cy, 8), cy)]
        return pltpu.make_async_remote_copy(
            src_ref=theirs,
            dst_ref=theirs,
            send_sem=g_send.at[kind, off - 1],
            recv_sem=g_recv.at[kind, off - 1],
            device_id=(gx, sender),
            device_id_type=MESH,
        )

    coarsen(
        [ext[COND, first + 2 * i, pl.ds(0, ny), :] + ext[COND, first + 2 * i + 1, pl.ds(0, ny), :]
         for i in range(cx)],
        0,
    )
    for off in range(1, n_gy):
        gather(0, off).start()

    receive(COND)
    join(COND)
    row = lax.broadcasted_iota(jnp.int32, (rows, 1), 0)
    y = gy * ny + jnp.where(row < ny + HALF, row, row - rows)
    in_y = jnp.where((y >= 0) & (y < n_gy * ny), RELAX_WEIGHT, 0.0)
    for i in range(first - 2, last + 2):
        cond = ext[COND, i]
        mixed = blend(ext[COND, i - 1], cond, ext[COND, i + 1])
        x = gx * nx + (i - first)
        in_x = jnp.where((x >= 0) & (x < n_gx * nx), 1.0, 0.0)
        weight[i] = (in_y * in_x) / (MASS_TERM + 6.0 * cond + mixed)
        diag2[i] = MASS_TERM + 8.0 * cond + mixed

    def defect(kind, i, values, flux):
        lhs = ext[COND, i] * blend(values[i - 1], values[i], values[i + 1])
        return ext[SOURCE, i] - diag2[i] * values[i] + lhs + blend(flux[i - 1], flux[i], flux[i + 1])

    receive(SOURCE)
    join(SOURCE)
    values, flux = {}, {}
    for i in range(first - 2, last + 2):
        values[i] = weight[i] * ext[SOURCE, i]
        flux[i] = ext[COND, i] * values[i]
    smooth = {}
    for i in range(first - 1, last + 1):
        smooth[i] = values[i] + weight[i] * defect(SOURCE, i, values, flux)
    flux = {i: ext[COND, i] * smooth[i] for i in smooth}
    pairs = []
    for i in range(cx):
        j = first + 2 * i
        pairs.append(
            defect(SOURCE, j, smooth, flux)[:ny] + defect(SOURCE, j + 1, smooth, flux)[:ny]
        )
    coarsen(pairs, 1)
    for off in range(1, n_gy):
        gather(1, off).start()
    for i in range(first, last):
        ext[ITERATE, i, pl.ds(0, ny), :] = smooth[i][:ny]
    pack(ITERATE)
    send(ITERATE)

    all_y = n_gy * cy
    crow = lax.broadcasted_iota(jnp.int32, (all_y, cz), 0)
    clane = lax.broadcasted_iota(jnp.int32, (all_y, cz), 1)
    owner = jnp.full((all_y, cz), owners_ref[0, 0], jnp.int32)
    for c in range(1, n_gy):
        owner = jnp.where(crow >= c * cy, owners_ref[0, c], owner)
    mask = jnp.where(owner == owners_ref[0, gy], 1.0, 0.0)
    y_low = jnp.where(crow == 0, 0.0, 0.5)
    y_high = jnp.where(crow == all_y - 1, 0.0, 0.5)
    cz_low = jnp.where(clane == 0, 0.0, 0.5)
    cz_high = jnp.where(clane == cz - 1, 0.0, 0.5)

    def coarse_blend(planes):
        mixed = []
        for i, u in enumerate(planes):
            if i > 0:
                u = u + 0.5 * planes[i - 1]
            if i + 1 < cx:
                u = u + 0.5 * planes[i + 1]
            u = u + y_low * pltpu.roll(u, 1, 0) + y_high * pltpu.roll(u, all_y - 1, 0)
            mixed.append(u + cz_low * pltpu.roll(u, 1, 1) + cz_high * pltpu.roll(u, cz - 1, 1))
        return mixed

    for off in range(1, n_gy):
        gather_in(0, off).wait_recv()
    cond_c = [mask * group[0, i] for i in range(cx)]
    mixed = coarse_blend(cond_c)
    diag_c = [MASS_TERM + 1.5 * k + 0.25 * b for k, b in zip(cond_c, mixed)]
    weight_c = [RELAX_WEIGHT * mask / d for d in diag_c]
    diag_sum = jnp.sum(functools.reduce(jnp.add, [mask * d for d in diag_c]), keepdims=True)

    for off in range(1, n_gy):
        gather_in(1, off).wait_recv()
    res_c = [mask * group[1, i] for i in range(cx)]

    def coarse_defect(e):
        straight = coarse_blend(e)
        carried = coarse_blend([k * v for k, v in zip(cond_c, e)])
        return [
            res_c[i] - (diag_c[i] + 0.5 * cond_c[i]) * e[i]
            + 0.25 * (cond_c[i] * straight[i] + carried[i])
            for i in range(cx)
        ]

    e = [w * r for w, r in zip(weight_c, res_c)]
    for _ in range(COARSE_SWEEPS - 1):
        d = coarse_defect(e)
        e = [e[i] + weight_c[i] * d[i] for i in range(cx)]
    d = coarse_defect(e)
    left = jnp.sum(functools.reduce(jnp.add, [mask * v for v in d]), keepdims=True)
    ratio = left / jnp.maximum(diag_sum, 1.0)
    for i in range(cx):
        whole_corr[i] = e[i] + mask * ratio
        corr[1 + i] = whole_corr[i, pl.ds(pl.multiple_of(gy * cy, 8), cy), :]
    for which, (dx, dy) in enumerate(STEPS):
        @pl.when(exists(dx, dy))
        def _():
            remote_corr(which).start()

    receive(ITERATE)
    join(ITERATE)
    for which, (dx, dy) in enumerate(STEPS):
        @pl.when(exists(-dx, -dy))
        def _():
            remote_corr(which).wait_recv()

    for i in range(cx + 2):
        mine = corr[i]
        spread[i, pl.ds(0, cy, stride=2), :] = mine
        spread[i, pl.ds(1, cy, stride=2), :] = mine
        for r in range(0, rows, 8):
            if r < ny:
                tile = spread[i, pl.ds(r, 8), :]
            else:
                tile = jnp.where(
                    lax.broadcasted_iota(jnp.int32, (8, cz), 0) < HALF,
                    jnp.broadcast_to(corr_y[0, i, pl.ds(0, 1), :], (8, cz)),
                    jnp.broadcast_to(corr_y[1, i, pl.ds(7, 1), :], (8, cz)),
                )
            for part in range(2):
                wide[i, pl.ds(r, 8), pl.ds(128 * part, 128)] = jnp.take_along_axis(
                    tile, half_of + 64 * part, axis=1
                )
    values = {
        i: ext[ITERATE, i] + wide[(i - first + 2) // 2] for i in range(first - 2, last + 2)
    }
    for sweep in range(POST_SWEEPS):
        reach = POST_SWEEPS - 1 - sweep
        flux = {i: ext[COND, i] * values[i] for i in values}
        values = {
            i: values[i] + weight[i] * defect(ITERATE, i, values, flux)
            for i in range(first - reach, last + reach)
        }
    stores = []
    for i in range(nx):
        result[i] = values[first + i][:ny]
        stores.append(pltpu.make_async_copy(result.at[i], out_ref.at[i], out_sem.at[i]))
        stores[i].start()

    for kind in range(3):
        finish(kind)
    for which, (dx, dy) in enumerate(STEPS):
        @pl.when(exists(dx, dy))
        def _():
            remote_corr(which).wait_send()

    for kind in range(2):
        for off in range(1, n_gy):
            gather(kind, off).wait_send()
    for store in stores:
        store.wait()


def on_device(source, region, permeability, owners, *, n_gx, n_gy):
    nx, ny, nz = source.shape
    planes = nx + 2 * WIDE
    f32 = jnp.float32
    return pl.pallas_call(
        functools.partial(kernel, n_gx, n_gy),
        out_shape=jax.ShapeDtypeStruct(source.shape, f32),
        in_specs=[
            pl.BlockSpec(memory_space=pltpu.HBM),
            pl.BlockSpec(memory_space=pltpu.HBM),
            pl.BlockSpec(memory_space=pltpu.HBM),
            pl.BlockSpec(memory_space=pltpu.HBM),
        ],
        out_specs=pl.BlockSpec(memory_space=pltpu.HBM),
        scratch_shapes=[
            pltpu.SMEM((1, n_gy), jnp.int32),
            pltpu.VMEM((1, permeability.shape[0]), f32),
            pltpu.VMEM((3, planes, ny + 8, nz), f32),
            pltpu.VMEM((3, 2, nx // 2, 8, nz), f32),
            pltpu.VMEM((3, nx // 2 + 4, 8, nz), f32),
            pltpu.VMEM((3, nx // 2 + 4, 8, nz), f32),
            pltpu.VMEM((nx, ny, nz), jnp.int32),
            pltpu.VMEM((planes, ny + 8, nz), f32),
            pltpu.VMEM((planes, ny + 8, nz), f32),
            pltpu.VMEM((nx, ny, nz), f32),
            pltpu.VMEM((2, nx // 2, n_gy * ny // 2, nz // 2), f32),
            pltpu.VMEM((nx // 2, ny, nz // 2), f32),
            pltpu.VMEM((nx // 2, n_gy * ny // 2, nz // 2), f32),
            pltpu.VMEM((nx // 2 + 2, ny, nz // 2), f32),
            pltpu.VMEM((nx // 2 + 2, ny // 2, nz // 2), f32),
            pltpu.VMEM((2, nx // 2 + 2, 8, nz // 2), f32),
            pltpu.VMEM((nx // 2 + 2, ny + 8, nz), f32),
            pltpu.SemaphoreType.DMA((3, 8)),
            pltpu.SemaphoreType.DMA((3, 8)),
            pltpu.SemaphoreType.DMA((2, n_gy - 1)),
            pltpu.SemaphoreType.DMA((2, n_gy - 1)),
            pltpu.SemaphoreType.DMA((4,)),
            pltpu.SemaphoreType.DMA((nx,)),
            pltpu.SemaphoreType.DMA((8,)),
            pltpu.SemaphoreType.DMA((8,)),
        ],
        compiler_params=pltpu.CompilerParams(
            collective_id=0, has_side_effects=True, vmem_limit_bytes=60 * 1024 * 1024
        ),
    )(owners, permeability[None, :], source, region)


def solution(mesh):
    placed = (P("gx", "gy", None), P("gx", "gy", None), P(), P("gx", None))
    body = functools.partial(on_device, n_gx=mesh.shape["gx"], n_gy=mesh.shape["gy"])
    return jax.shard_map(
        body, mesh=mesh, in_specs=placed, out_specs=P("gx", "gy", None), check_vma=False
    )
```

```python
import functools

import jax
import jax.numpy as jnp
from jax import lax
from jax.experimental import pallas as pl
from jax.experimental.pallas import tpu as pltpu
from jax.sharding import PartitionSpec as P

POST_SWEEPS = 2
COARSE_SWEEPS = 6
RELAX_WEIGHT = 0.6
MASS_TERM = 0.1

MESH = pl.DeviceIdType.MESH
WIDE = 3
HALF = 4
COND, SOURCE, ITERATE = 0, 1, 2
WIDTHS = (3, 2, 2)
STEPS = ((-1, 0), (1, 0), (0, -1), (0, 1), (-1, -1), (1, -1), (-1, 1), (1, 1))


def kernel(
    n_gx, n_gy,
    owners_in, table_in, source_ref, region_ref, out_ref,
    owners_ref, table_ref, ext, packed, after, before, labels, weight, diag2, result, group, squeezed, whole_corr, spread, corr, corr_y, wide,
    send_sem, recv_sem, g_send, g_recv, in_sem, out_sem, c_send, c_recv,
):
    nx, ny, nz = out_ref.shape
    cx, cy, cz = nx // 2, ny // 2, nz // 2
    first, last = WIDE, WIDE + nx
    gx, gy = lax.axis_index("gx"), lax.axis_index("gy")

    def exists(dx, dy):
        x, y = gx + dx, gy + dy
        return (x >= 0) & (x < n_gx) & (y >= 0) & (y < n_gy)

    load_source = pltpu.make_async_copy(
        source_ref, ext.at[SOURCE, pl.ds(first, nx), pl.ds(0, ny)], in_sem.at[0]
    )
    load_region = pltpu.make_async_copy(region_ref, labels, in_sem.at[1])
    load_table = pltpu.make_async_copy(table_in, table_ref, in_sem.at[2])
    load_owners = pltpu.make_async_copy(owners_in, owners_ref, in_sem.at[3])
    load_region.start()
    load_table.start()
    load_source.start()
    load_owners.start()

    barrier = pltpu.get_barrier_semaphore()
    count = jnp.int32(0)
    for dx, dy in STEPS:
        near = exists(dx, dy)

        @pl.when(near)
        def _():
            pl.semaphore_signal(
                barrier, inc=1, device_id=(gx + dx, gy + dy), device_id_type=MESH
            )

        count = count + near.astype(jnp.int32)
    for off in range(2 - n_gy - 1, n_gy):
        if abs(off) >= 2:
            near = exists(0, off)

            @pl.when(near)
            def _():
                pl.semaphore_signal(
                    barrier, inc=1, device_id=(gx, gy + off), device_id_type=MESH
                )

            count = count + near.astype(jnp.int32)

    def planes_in(dx, w):
        return {0: (first, nx), -1: (last, w), 1: (first - w, w)}[dx]

    def planes_out(dx, w):
        return {0: (first, nx), -1: (first, w), 1: (last - w, w)}[dx]

    def landing(kind, dx, dy, w):
        start, size = planes_in(dx, w)
        if dy == 0:
            return ext.at[kind, pl.ds(start, size), pl.ds(0, ny)]
        start, size = {0: (2, cx), -1: (2 + cx, (w + 1) // 2), 1: (2 - (w + 1) // 2, (w + 1) // 2)}[dx]
        return (after if dy < 0 else before).at[kind, pl.ds(start, size)]

    def remote(kind, which):
        dx, dy = STEPS[which]
        w = WIDTHS[kind]
        start, size = planes_out(dx, w)
        if dy == 0:
            source = ext.at[kind, pl.ds(start, size), pl.ds(0, ny)]
        else:
            tiles = (w + 1) // 2
            start, size = {0: (0, cx), -1: (0, tiles), 1: (cx - tiles, tiles)}[dx]
            source = packed.at[kind, max(dy, 0), pl.ds(start, size)]
        return pltpu.make_async_remote_copy(
            src_ref=source,
            dst_ref=landing(kind, dx, dy, w),
            send_sem=send_sem.at[kind, which],
            recv_sem=recv_sem.at[kind, which],
            device_id=(gx + dx, gy + dy),
            device_id_type=MESH,
        )

    def landing_corr(dx, dy):
        at = {0: pl.ds(1, cx), -1: pl.ds(cx + 1, 1), 1: pl.ds(0, 1)}[dx]
        return corr.at[at] if dy == 0 else corr_y.at[max(dy, 0), at]

    def remote_corr(which):
        dx, dy = STEPS[which]
        at = {0: pl.ds(1, cx), -1: pl.ds(1, 1), 1: pl.ds(cx, 1)}[dx]
        rows = {0: pl.ds(0, cy), -1: pl.ds(0, 8), 1: pl.ds(cy - 8, 8)}[dy]
        return pltpu.make_async_remote_copy(
            src_ref=corr.at[at, rows],
            dst_ref=landing_corr(dx, dy),
            send_sem=c_send.at[which],
            recv_sem=c_recv.at[which],
            device_id=(gx + dx, gy + dy),
            device_id_type=MESH,
        )

    def send(kind):
        for which, (dx, dy) in enumerate(STEPS):
            @pl.when(exists(dx, dy))
            def _():
                remote(kind, which).start()

    def receive(kind):
        for which, (dx, dy) in enumerate(STEPS):
            @pl.when(exists(-dx, -dy))
            def _():
                remote(kind, which).wait_recv()

    def finish(kind):
        for which, (dx, dy) in enumerate(STEPS):
            @pl.when(exists(dx, dy))
            def _():
                remote(kind, which).wait_send()

    for dx, dy in STEPS:
        @pl.when(jnp.logical_not(exists(-dx, -dy)))
        def _():
            for kind in range(3):
                ref = landing(kind, dx, dy, WIDTHS[kind])
                ref[...] = jnp.zeros(ref.shape, jnp.float32)
            ref = landing_corr(dx, dy)
            ref[...] = jnp.zeros(ref.shape, jnp.float32)

    row8 = lax.broadcasted_iota(jnp.int32, (8, nz), 0)

    def pack(kind):
        for s in range(cx):
            a, b = first + 2 * s, first + 2 * s + 1
            packed[kind, 0, s] = jnp.where(
                row8 < HALF, ext[kind, a, pl.ds(0, 8), :],
                pltpu.roll(ext[kind, b, pl.ds(0, 8), :], HALF, 0),
            )
            packed[kind, 1, s] = jnp.where(
                row8 < HALF, pltpu.roll(ext[kind, a, pl.ds(ny - 8, 8), :], HALF, 0),
                ext[kind, b, pl.ds(ny - 8, 8), :],
            )

    def join(kind):
        w = WIDTHS[kind]
        for i in range(first - w, last + w):
            s, odd = divmod(i - first + 4, 2)
            low, high = after[kind, s], before[kind, s]
            if odd:
                low = pltpu.roll(low, HALF, 0)
            else:
                high = pltpu.roll(high, HALF, 0)
            ext[kind, i, pl.ds(ny, 8), :] = jnp.where(row8 < HALF, low, high)

    load_table.wait()
    load_region.wait()
    pair = jnp.concatenate([table_ref[...], table_ref[...]], axis=1)
    table = jnp.broadcast_to(pair, (8, 128))
    for i in range(nx):
        for r in range(0, ny, 8):
            for c in range(0, nz, 128):
                spot = labels[i, pl.ds(r, 8), pl.ds(c, 128)]
                ext[COND, first + i, pl.ds(r, 8), pl.ds(c, 128)] = jnp.take_along_axis(
                    table, spot, axis=1
                )

    pack(COND)
    pl.semaphore_wait(barrier, count)
    send(COND)
    load_source.wait()
    pack(SOURCE)
    send(SOURCE)
    load_owners.wait()

    lane = lax.broadcasted_iota(jnp.int32, (1, nz), 1)
    z_low = jnp.where(lane == 0, 0.0, 0.5)
    z_high = jnp.where(lane == nz - 1, 0.0, 0.5)
    rows = ny + 8

    def blend(a, b, c, keep=rows):
        u = b + 0.5 * (a + c)
        u = u + 0.5 * (pltpu.roll(u, 1, 0) + pltpu.roll(u, rows - 1, 0))
        u = u[:keep]
        return u + z_low * pltpu.roll(u, 1, 1) + z_high * pltpu.roll(u, nz - 1, 1)

    lane128 = lax.broadcasted_iota(jnp.int32, (8, 128), 1)
    even = lax.rem(2 * lane128, jnp.int32(128))
    half_of = lane128 // 2

    def coarsen(pairs, kind):
        for i, pair_sum in enumerate(pairs):
            total = pair_sum + pltpu.roll(pair_sum, nz - 1, 1)
            for r in range(0, ny, 8):
                low = jnp.take_along_axis(total[r:r + 8, :128], even, axis=1)
                high = jnp.take_along_axis(total[r:r + 8, 128:], even, axis=1)
                squeezed[i, pl.ds(r, 8), :] = jnp.where(lane128 < 64, low, high)
            block = squeezed[i, pl.ds(0, cy, stride=2), :] + squeezed[i, pl.ds(1, cy, stride=2), :]
            group[kind, i, pl.ds(pl.multiple_of(gy * cy, 8), cy), :] = 0.125 * block

    def gather(kind, off):
        mine = group.at[kind, :, pl.ds(pl.multiple_of(gy * cy, 8), cy)]
        return pltpu.make_async_remote_copy(
            src_ref=mine,
            dst_ref=mine,
            send_sem=g_send.at[kind, off - 1],
            recv_sem=g_recv.at[kind, off - 1],
            device_id=(gx, lax.rem(gy + off, n_gy)),
            device_id_type=MESH,
        )

    def gather_in(kind, off):
        sender = lax.rem(gy + n_gy - off, n_gy)
        theirs = group.at[kind, :, pl.ds(pl.multiple_of(sender * cy, 8), cy)]
        return pltpu.make_async_remote_copy(
            src_ref=theirs,
            dst_ref=theirs,
            send_sem=g_send.at[kind, off - 1],
            recv_sem=g_recv.at[kind, off - 1],
            device_id=(gx, sender),
            device_id_type=MESH,
        )

    coarsen(
        [ext[COND, first + 2 * i, pl.ds(0, ny), :] + ext[COND, first + 2 * i + 1, pl.ds(0, ny), :]
         for i in range(cx)],
        0,
    )
    for off in range(1, n_gy):
        gather(0, off).start()

    receive(COND)
    join(COND)
    row = lax.broadcasted_iota(jnp.int32, (rows, 1), 0)
    y = gy * ny + jnp.where(row < ny + HALF, row, row - rows)
    in_y = jnp.where((y >= 0) & (y < n_gy * ny), RELAX_WEIGHT, 0.0)
    for i in range(first - 2, last + 2):
        cond = ext[COND, i]
        mixed = blend(ext[COND, i - 1], cond, ext[COND, i + 1])
        x = gx * nx + (i - first)
        in_x = jnp.where((x >= 0) & (x < n_gx * nx), 1.0, 0.0)
        weight[i] = (in_y * in_x) / (MASS_TERM + 6.0 * cond + mixed)
        diag2[i] = MASS_TERM + 8.0 * cond + mixed

    def defect(kind, i, values, flux, keep=rows):
        at = pl.ds(0, keep)
        lhs = ext[COND, i, at] * blend(values[i - 1], values[i], values[i + 1], keep)
        rhs = blend(flux[i - 1], flux[i], flux[i + 1], keep)
        return ext[SOURCE, i, at] - diag2[i, at] * values[i][:keep] + lhs + rhs

    receive(SOURCE)
    join(SOURCE)
    values, flux = {}, {}
    for i in range(first - 2, last + 2):
        values[i] = weight[i] * ext[SOURCE, i]
        flux[i] = ext[COND, i] * values[i]
    smooth = {}
    for i in range(first - 1, last + 1):
        smooth[i] = values[i] + weight[i] * defect(SOURCE, i, values, flux)
    flux = {i: ext[COND, i] * smooth[i] for i in smooth}
    pairs = []
    for i in range(cx):
        j = first + 2 * i
        pairs.append(
            defect(SOURCE, j, smooth, flux, ny) + defect(SOURCE, j + 1, smooth, flux, ny)
        )
    coarsen(pairs, 1)
    for off in range(1, n_gy):
        gather(1, off).start()
    for i in range(first, last):
        ext[ITERATE, i, pl.ds(0, ny), :] = smooth[i][:ny]
    pack(ITERATE)
    send(ITERATE)

    all_y = n_gy * cy
    crow = lax.broadcasted_iota(jnp.int32, (all_y, cz), 0)
    clane = lax.broadcasted_iota(jnp.int32, (all_y, cz), 1)
    owner = jnp.full((all_y, cz), owners_ref[0, 0], jnp.int32)
    for c in range(1, n_gy):
        owner = jnp.where(crow >= c * cy, owners_ref[0, c], owner)
    mask = jnp.where(owner == owners_ref[0, gy], 1.0, 0.0)
    y_low = jnp.where(crow == 0, 0.0, 0.5)
    y_high = jnp.where(crow == all_y - 1, 0.0, 0.5)
    cz_low = jnp.where(clane == 0, 0.0, 0.5)
    cz_high = jnp.where(clane == cz - 1, 0.0, 0.5)

    def coarse_blend(planes):
        mixed = []
        for i, u in enumerate(planes):
            if i > 0:
                u = u + 0.5 * planes[i - 1]
            if i + 1 < cx:
                u = u + 0.5 * planes[i + 1]
            u = u + y_low * pltpu.roll(u, 1, 0) + y_high * pltpu.roll(u, all_y - 1, 0)
            mixed.append(u + cz_low * pltpu.roll(u, 1, 1) + cz_high * pltpu.roll(u, cz - 1, 1))
        return mixed

    for off in range(1, n_gy):
        gather_in(0, off).wait_recv()
    cond_c = [mask * group[0, i] for i in range(cx)]
    mixed = coarse_blend(cond_c)
    diag_c = [MASS_TERM + 1.5 * k + 0.25 * b for k, b in zip(cond_c, mixed)]
    weight_c = [RELAX_WEIGHT * mask / d for d in diag_c]
    diag_sum = jnp.sum(functools.reduce(jnp.add, [mask * d for d in diag_c]), keepdims=True)

    for off in range(1, n_gy):
        gather_in(1, off).wait_recv()
    res_c = [mask * group[1, i] for i in range(cx)]

    def coarse_defect(e):
        straight = coarse_blend(e)
        carried = coarse_blend([k * v for k, v in zip(cond_c, e)])
        return [
            res_c[i] - (diag_c[i] + 0.5 * cond_c[i]) * e[i]
            + 0.25 * (cond_c[i] * straight[i] + carried[i])
            for i in range(cx)
        ]

    e = [w * r for w, r in zip(weight_c, res_c)]
    for _ in range(COARSE_SWEEPS - 1):
        d = coarse_defect(e)
        e = [e[i] + weight_c[i] * d[i] for i in range(cx)]
    d = coarse_defect(e)
    left = jnp.sum(functools.reduce(jnp.add, [mask * v for v in d]), keepdims=True)
    ratio = left / jnp.maximum(diag_sum, 1.0)
    for i in range(cx):
        whole_corr[i] = e[i] + mask * ratio
        corr[1 + i] = whole_corr[i, pl.ds(pl.multiple_of(gy * cy, 8), cy), :]
    for which, (dx, dy) in enumerate(STEPS):
        @pl.when(exists(dx, dy))
        def _():
            remote_corr(which).start()

    receive(ITERATE)
    join(ITERATE)
    for which, (dx, dy) in enumerate(STEPS):
        @pl.when(exists(-dx, -dy))
        def _():
            remote_corr(which).wait_recv()

    for i in range(cx + 2):
        mine = corr[i]
        spread[i, pl.ds(0, cy, stride=2), :] = mine
        spread[i, pl.ds(1, cy, stride=2), :] = mine
        for r in range(0, rows, 8):
            if r < ny:
                tile = spread[i, pl.ds(r, 8), :]
            else:
                tile = jnp.where(
                    lax.broadcasted_iota(jnp.int32, (8, cz), 0) < HALF,
                    jnp.broadcast_to(corr_y[0, i, pl.ds(0, 1), :], (8, cz)),
                    jnp.broadcast_to(corr_y[1, i, pl.ds(7, 1), :], (8, cz)),
                )
            for part in range(2):
                wide[i, pl.ds(r, 8), pl.ds(128 * part, 128)] = jnp.take_along_axis(
                    tile, half_of + 64 * part, axis=1
                )
    values = {
        i: ext[ITERATE, i] + wide[(i - first + 2) // 2] for i in range(first - 2, last + 2)
    }
    for sweep in range(POST_SWEEPS):
        reach = POST_SWEEPS - 1 - sweep
        keep = rows if reach else ny
        flux = {i: ext[COND, i] * values[i] for i in values}
        values = {
            i: values[i][:keep] + weight[i, pl.ds(0, keep)] * defect(ITERATE, i, values, flux, keep)
            for i in range(first - reach, last + reach)
        }
    stores = []
    for i in range(nx):
        result[i] = values[first + i][:ny]
        stores.append(pltpu.make_async_copy(result.at[i], out_ref.at[i], out_sem.at[i]))
        stores[i].start()

    for kind in range(3):
        finish(kind)
    for which, (dx, dy) in enumerate(STEPS):
        @pl.when(exists(dx, dy))
        def _():
            remote_corr(which).wait_send()

    for kind in range(2):
        for off in range(1, n_gy):
            gather(kind, off).wait_send()
    for store in stores:
        store.wait()


def on_device(source, region, permeability, owners, *, n_gx, n_gy):
    nx, ny, nz = source.shape
    planes = nx + 2 * WIDE
    f32 = jnp.float32
    return pl.pallas_call(
        functools.partial(kernel, n_gx, n_gy),
        out_shape=jax.ShapeDtypeStruct(source.shape, f32),
        in_specs=[
            pl.BlockSpec(memory_space=pltpu.HBM),
            pl.BlockSpec(memory_space=pltpu.HBM),
            pl.BlockSpec(memory_space=pltpu.HBM),
            pl.BlockSpec(memory_space=pltpu.HBM),
        ],
        out_specs=pl.BlockSpec(memory_space=pltpu.HBM),
        scratch_shapes=[
            pltpu.SMEM((1, n_gy), jnp.int32),
            pltpu.VMEM((1, permeability.shape[0]), f32),
            pltpu.VMEM((3, planes, ny + 8, nz), f32),
            pltpu.VMEM((3, 2, nx // 2, 8, nz), f32),
            pltpu.VMEM((3, nx // 2 + 4, 8, nz), f32),
            pltpu.VMEM((3, nx // 2 + 4, 8, nz), f32),
            pltpu.VMEM((nx, ny, nz), jnp.int32),
            pltpu.VMEM((planes, ny + 8, nz), f32),
            pltpu.VMEM((planes, ny + 8, nz), f32),
            pltpu.VMEM((nx, ny, nz), f32),
            pltpu.VMEM((2, nx // 2, n_gy * ny // 2, nz // 2), f32),
            pltpu.VMEM((nx // 2, ny, nz // 2), f32),
            pltpu.VMEM((nx // 2, n_gy * ny // 2, nz // 2), f32),
            pltpu.VMEM((nx // 2 + 2, ny, nz // 2), f32),
            pltpu.VMEM((nx // 2 + 2, ny // 2, nz // 2), f32),
            pltpu.VMEM((2, nx // 2 + 2, 8, nz // 2), f32),
            pltpu.VMEM((nx // 2 + 2, ny + 8, nz), f32),
            pltpu.SemaphoreType.DMA((3, 8)),
            pltpu.SemaphoreType.DMA((3, 8)),
            pltpu.SemaphoreType.DMA((2, n_gy - 1)),
            pltpu.SemaphoreType.DMA((2, n_gy - 1)),
            pltpu.SemaphoreType.DMA((4,)),
            pltpu.SemaphoreType.DMA((nx,)),
            pltpu.SemaphoreType.DMA((8,)),
            pltpu.SemaphoreType.DMA((8,)),
        ],
        compiler_params=pltpu.CompilerParams(
            collective_id=0, has_side_effects=True, vmem_limit_bytes=60 * 1024 * 1024
        ),
    )(owners, permeability[None, :], source, region)


def solution(mesh):
    placed = (P("gx", "gy", None), P("gx", "gy", None), P(), P("gx", None))
    body = functools.partial(on_device, n_gx=mesh.shape["gx"], n_gy=mesh.shape["gy"])
    return jax.shard_map(
        body, mesh=mesh, in_specs=placed, out_specs=P("gx", "gy", None), check_vma=False
    )
```

```python
import functools

import jax
import jax.numpy as jnp
from jax import lax
from jax.experimental import pallas as pl
from jax.experimental.pallas import tpu as pltpu
from jax.sharding import PartitionSpec as P

POST_SWEEPS = 2
COARSE_SWEEPS = 6
RELAX_WEIGHT = 0.6
MASS_TERM = 0.1

MESH = pl.DeviceIdType.MESH
WIDE = 3
HALF = 4
COND, SOURCE, ITERATE = 0, 1, 2
WIDTHS = (3, 2, 2)
STEPS = ((-1, 0), (1, 0), (0, -1), (0, 1), (-1, -1), (1, -1), (-1, 1), (1, 1))


def kernel(
    n_gx, n_gy,
    owners_in, table_in, source_ref, region_ref, out_ref,
    owners_ref, table_ref, ext, packed, after, before, labels, weight, diag2, group, squeezed, whole_corr, spread, corr, corr_y, wide,
    send_sem, recv_sem, g_send, g_recv, in_sem, c_send, c_recv,
):
    nx, ny, nz = out_ref.shape
    cx, cy, cz = nx // 2, ny // 2, nz // 2
    first, last = WIDE, WIDE + nx
    gx, gy = lax.axis_index("gx"), lax.axis_index("gy")

    def exists(dx, dy):
        x, y = gx + dx, gy + dy
        return (x >= 0) & (x < n_gx) & (y >= 0) & (y < n_gy)

    load_source = pltpu.make_async_copy(
        source_ref, ext.at[SOURCE, pl.ds(first, nx), pl.ds(0, ny)], in_sem.at[0]
    )
    load_region = pltpu.make_async_copy(region_ref, labels, in_sem.at[1])
    load_table = pltpu.make_async_copy(table_in, table_ref, in_sem.at[2])
    load_owners = pltpu.make_async_copy(owners_in, owners_ref, in_sem.at[3])
    load_region.start()
    load_table.start()
    load_source.start()
    load_owners.start()

    barrier = pltpu.get_barrier_semaphore()
    count = jnp.int32(0)
    for dx, dy in STEPS:
        near = exists(dx, dy)

        @pl.when(near)
        def _():
            pl.semaphore_signal(
                barrier, inc=1, device_id=(gx + dx, gy + dy), device_id_type=MESH
            )

        count = count + near.astype(jnp.int32)
    for off in range(2 - n_gy - 1, n_gy):
        if abs(off) >= 2:
            near = exists(0, off)

            @pl.when(near)
            def _():
                pl.semaphore_signal(
                    barrier, inc=1, device_id=(gx, gy + off), device_id_type=MESH
                )

            count = count + near.astype(jnp.int32)

    def planes_in(dx, w):
        return {0: (first, nx), -1: (last, w), 1: (first - w, w)}[dx]

    def planes_out(dx, w):
        return {0: (first, nx), -1: (first, w), 1: (last - w, w)}[dx]

    def landing(kind, dx, dy, w):
        start, size = planes_in(dx, w)
        if dy == 0:
            return ext.at[kind, pl.ds(start, size), pl.ds(0, ny)]
        start, size = {0: (2, cx), -1: (2 + cx, (w + 1) // 2), 1: (2 - (w + 1) // 2, (w + 1) // 2)}[dx]
        return (after if dy < 0 else before).at[kind, pl.ds(start, size)]

    def remote(kind, which):
        dx, dy = STEPS[which]
        w = WIDTHS[kind]
        start, size = planes_out(dx, w)
        if dy == 0:
            source = ext.at[kind, pl.ds(start, size), pl.ds(0, ny)]
        else:
            tiles = (w + 1) // 2
            start, size = {0: (0, cx), -1: (0, tiles), 1: (cx - tiles, tiles)}[dx]
            source = packed.at[kind, max(dy, 0), pl.ds(start, size)]
        return pltpu.make_async_remote_copy(
            src_ref=source,
            dst_ref=landing(kind, dx, dy, w),
            send_sem=send_sem.at[kind, which],
            recv_sem=recv_sem.at[kind, which],
            device_id=(gx + dx, gy + dy),
            device_id_type=MESH,
        )

    def landing_corr(dx, dy):
        at = {0: pl.ds(1, cx), -1: pl.ds(cx + 1, 1), 1: pl.ds(0, 1)}[dx]
        return corr.at[at] if dy == 0 else corr_y.at[max(dy, 0), at]

    def remote_corr(which):
        dx, dy = STEPS[which]
        at = {0: pl.ds(1, cx), -1: pl.ds(1, 1), 1: pl.ds(cx, 1)}[dx]
        rows = {0: pl.ds(0, cy), -1: pl.ds(0, 8), 1: pl.ds(cy - 8, 8)}[dy]
        return pltpu.make_async_remote_copy(
            src_ref=corr.at[at, rows],
            dst_ref=landing_corr(dx, dy),
            send_sem=c_send.at[which],
            recv_sem=c_recv.at[which],
            device_id=(gx + dx, gy + dy),
            device_id_type=MESH,
        )

    def send(kind):
        for which, (dx, dy) in enumerate(STEPS):
            @pl.when(exists(dx, dy))
            def _():
                remote(kind, which).start()

    def receive(kind):
        for which, (dx, dy) in enumerate(STEPS):
            @pl.when(exists(-dx, -dy))
            def _():
                remote(kind, which).wait_recv()

    def finish(kind):
        for which, (dx, dy) in enumerate(STEPS):
            @pl.when(exists(dx, dy))
            def _():
                remote(kind, which).wait_send()

    for dx, dy in STEPS:
        @pl.when(jnp.logical_not(exists(-dx, -dy)))
        def _():
            for kind in range(3):
                ref = landing(kind, dx, dy, WIDTHS[kind])
                ref[...] = jnp.zeros(ref.shape, jnp.float32)
            ref = landing_corr(dx, dy)
            ref[...] = jnp.zeros(ref.shape, jnp.float32)

    row8 = lax.broadcasted_iota(jnp.int32, (8, nz), 0)

    def pack(kind):
        for s in range(cx):
            a, b = first + 2 * s, first + 2 * s + 1
            packed[kind, 0, s] = jnp.where(
                row8 < HALF, ext[kind, a, pl.ds(0, 8), :],
                pltpu.roll(ext[kind, b, pl.ds(0, 8), :], HALF, 0),
            )
            packed[kind, 1, s] = jnp.where(
                row8 < HALF, pltpu.roll(ext[kind, a, pl.ds(ny - 8, 8), :], HALF, 0),
                ext[kind, b, pl.ds(ny - 8, 8), :],
            )

    def join(kind):
        w = WIDTHS[kind]
        for i in range(first - w, last + w):
            s, odd = divmod(i - first + 4, 2)
            low, high = after[kind, s], before[kind, s]
            if odd:
                low = pltpu.roll(low, HALF, 0)
            else:
                high = pltpu.roll(high, HALF, 0)
            ext[kind, i, pl.ds(ny, 8), :] = jnp.where(row8 < HALF, low, high)

    load_table.wait()
    load_region.wait()
    pair = jnp.concatenate([table_ref[...], table_ref[...]], axis=1)
    table = jnp.broadcast_to(pair, (8, 128))
    for i in range(nx):
        for r in range(0, ny, 8):
            for c in range(0, nz, 128):
                spot = labels[i, pl.ds(r, 8), pl.ds(c, 128)]
                ext[COND, first + i, pl.ds(r, 8), pl.ds(c, 128)] = jnp.take_along_axis(
                    table, spot, axis=1
                )

    pack(COND)
    pl.semaphore_wait(barrier, count)
    send(COND)
    load_source.wait()
    pack(SOURCE)
    send(SOURCE)
    load_owners.wait()

    lane = lax.broadcasted_iota(jnp.int32, (1, nz), 1)
    z_low = jnp.where(lane == 0, 0.0, 0.5)
    z_high = jnp.where(lane == nz - 1, 0.0, 0.5)
    rows = ny + 8

    def blend(a, b, c, keep=rows):
        u = b + 0.5 * (a + c)
        u = u + 0.5 * (pltpu.roll(u, 1, 0) + pltpu.roll(u, rows - 1, 0))
        u = u[:keep]
        return u + z_low * pltpu.roll(u, 1, 1) + z_high * pltpu.roll(u, nz - 1, 1)

    lane128 = lax.broadcasted_iota(jnp.int32, (8, 128), 1)
    even = lax.rem(2 * lane128, jnp.int32(128))
    half_of = lane128 // 2

    def coarsen(pairs, kind):
        for i, pair_sum in enumerate(pairs):
            total = pair_sum + pltpu.roll(pair_sum, nz - 1, 1)
            for r in range(0, ny, 8):
                low = jnp.take_along_axis(total[r:r + 8, :128], even, axis=1)
                high = jnp.take_along_axis(total[r:r + 8, 128:], even, axis=1)
                squeezed[i, pl.ds(r, 8), :] = jnp.where(lane128 < 64, low, high)
            block = squeezed[i, pl.ds(0, cy, stride=2), :] + squeezed[i, pl.ds(1, cy, stride=2), :]
            group[kind, i, pl.ds(pl.multiple_of(gy * cy, 8), cy), :] = 0.125 * block

    def gather(kind, off):
        mine = group.at[kind, :, pl.ds(pl.multiple_of(gy * cy, 8), cy)]
        return pltpu.make_async_remote_copy(
            src_ref=mine,
            dst_ref=mine,
            send_sem=g_send.at[kind, off - 1],
            recv_sem=g_recv.at[kind, off - 1],
            device_id=(gx, lax.rem(gy + off, n_gy)),
            device_id_type=MESH,
        )

    def gather_in(kind, off):
        sender = lax.rem(gy + n_gy - off, n_gy)
        theirs = group.at[kind, :, pl.ds(pl.multiple_of(sender * cy, 8), cy)]
        return pltpu.make_async_remote_copy(
            src_ref=theirs,
            dst_ref=theirs,
            send_sem=g_send.at[kind, off - 1],
            recv_sem=g_recv.at[kind, off - 1],
            device_id=(gx, sender),
            device_id_type=MESH,
        )

    coarsen(
        [ext[COND, first + 2 * i, pl.ds(0, ny), :] + ext[COND, first + 2 * i + 1, pl.ds(0, ny), :]
         for i in range(cx)],
        0,
    )
    for off in range(1, n_gy):
        gather(0, off).start()

    receive(COND)
    join(COND)
    row = lax.broadcasted_iota(jnp.int32, (rows, 1), 0)
    y = gy * ny + jnp.where(row < ny + HALF, row, row - rows)
    in_y = jnp.where((y >= 0) & (y < n_gy * ny), RELAX_WEIGHT, 0.0)
    for i in range(first - 2, last + 2):
        cond = ext[COND, i]
        mixed = blend(ext[COND, i - 1], cond, ext[COND, i + 1])
        x = gx * nx + (i - first)
        in_x = jnp.where((x >= 0) & (x < n_gx * nx), 1.0, 0.0)
        weight[i] = (in_y * in_x) / (MASS_TERM + 6.0 * cond + mixed)
        diag2[i] = MASS_TERM + 8.0 * cond + mixed

    def defect(kind, i, values, flux, keep=rows):
        at = pl.ds(0, keep)
        lhs = ext[COND, i, at] * blend(values[i - 1], values[i], values[i + 1], keep)
        rhs = blend(flux[i - 1], flux[i], flux[i + 1], keep)
        return ext[SOURCE, i, at] - diag2[i, at] * values[i][:keep] + lhs + rhs

    receive(SOURCE)
    join(SOURCE)
    values, flux = {}, {}
    for i in range(first - 2, last + 2):
        values[i] = weight[i] * ext[SOURCE, i]
        flux[i] = ext[COND, i] * values[i]
    smooth = {}
    for i in range(first - 1, last + 1):
        smooth[i] = values[i] + weight[i] * defect(SOURCE, i, values, flux)
    flux = {i: ext[COND, i] * smooth[i] for i in smooth}
    pairs = []
    for i in range(cx):
        j = first + 2 * i
        pairs.append(
            defect(SOURCE, j, smooth, flux, ny) + defect(SOURCE, j + 1, smooth, flux, ny)
        )
    coarsen(pairs, 1)
    for off in range(1, n_gy):
        gather(1, off).start()
    for i in range(first, last):
        ext[ITERATE, i, pl.ds(0, ny), :] = smooth[i][:ny]
    pack(ITERATE)
    send(ITERATE)

    all_y = n_gy * cy
    crow = lax.broadcasted_iota(jnp.int32, (all_y, cz), 0)
    clane = lax.broadcasted_iota(jnp.int32, (all_y, cz), 1)
    owner = jnp.full((all_y, cz), owners_ref[0, 0], jnp.int32)
    for c in range(1, n_gy):
        owner = jnp.where(crow >= c * cy, owners_ref[0, c], owner)
    mask = jnp.where(owner == owners_ref[0, gy], 1.0, 0.0)
    y_low = jnp.where(crow == 0, 0.0, 0.5)
    y_high = jnp.where(crow == all_y - 1, 0.0, 0.5)
    cz_low = jnp.where(clane == 0, 0.0, 0.5)
    cz_high = jnp.where(clane == cz - 1, 0.0, 0.5)

    def coarse_blend(planes):
        mixed = []
        for i, u in enumerate(planes):
            if i > 0:
                u = u + 0.5 * planes[i - 1]
            if i + 1 < cx:
                u = u + 0.5 * planes[i + 1]
            u = u + y_low * pltpu.roll(u, 1, 0) + y_high * pltpu.roll(u, all_y - 1, 0)
            mixed.append(u + cz_low * pltpu.roll(u, 1, 1) + cz_high * pltpu.roll(u, cz - 1, 1))
        return mixed

    for off in range(1, n_gy):
        gather_in(0, off).wait_recv()
    cond_c = [mask * group[0, i] for i in range(cx)]
    mixed = coarse_blend(cond_c)
    diag_c = [MASS_TERM + 1.5 * k + 0.25 * b for k, b in zip(cond_c, mixed)]
    weight_c = [RELAX_WEIGHT * mask / d for d in diag_c]
    diag_sum = jnp.sum(functools.reduce(jnp.add, [mask * d for d in diag_c]), keepdims=True)

    for off in range(1, n_gy):
        gather_in(1, off).wait_recv()
    res_c = [mask * group[1, i] for i in range(cx)]

    def coarse_defect(e):
        straight = coarse_blend(e)
        carried = coarse_blend([k * v for k, v in zip(cond_c, e)])
        return [
            res_c[i] - (diag_c[i] + 0.5 * cond_c[i]) * e[i]
            + 0.25 * (cond_c[i] * straight[i] + carried[i])
            for i in range(cx)
        ]

    e = [w * r for w, r in zip(weight_c, res_c)]
    for _ in range(COARSE_SWEEPS - 1):
        d = coarse_defect(e)
        e = [e[i] + weight_c[i] * d[i] for i in range(cx)]
    d = coarse_defect(e)
    left = jnp.sum(functools.reduce(jnp.add, [mask * v for v in d]), keepdims=True)
    ratio = left / jnp.maximum(diag_sum, 1.0)
    for i in range(cx):
        whole_corr[i] = e[i] + mask * ratio
        corr[1 + i] = whole_corr[i, pl.ds(pl.multiple_of(gy * cy, 8), cy), :]
    for which, (dx, dy) in enumerate(STEPS):
        @pl.when(exists(dx, dy))
        def _():
            remote_corr(which).start()

    receive(ITERATE)
    join(ITERATE)
    for which, (dx, dy) in enumerate(STEPS):
        @pl.when(exists(-dx, -dy))
        def _():
            remote_corr(which).wait_recv()

    for i in range(cx + 2):
        mine = corr[i]
        spread[i, pl.ds(0, cy, stride=2), :] = mine
        spread[i, pl.ds(1, cy, stride=2), :] = mine
        for r in range(0, rows, 8):
            if r < ny:
                tile = spread[i, pl.ds(r, 8), :]
            else:
                tile = jnp.where(
                    lax.broadcasted_iota(jnp.int32, (8, cz), 0) < HALF,
                    jnp.broadcast_to(corr_y[0, i, pl.ds(0, 1), :], (8, cz)),
                    jnp.broadcast_to(corr_y[1, i, pl.ds(7, 1), :], (8, cz)),
                )
            for part in range(2):
                wide[i, pl.ds(r, 8), pl.ds(128 * part, 128)] = jnp.take_along_axis(
                    tile, half_of + 64 * part, axis=1
                )
    values = {
        i: ext[ITERATE, i] + wide[(i - first + 2) // 2] for i in range(first - 2, last + 2)
    }
    for sweep in range(POST_SWEEPS):
        reach = POST_SWEEPS - 1 - sweep
        keep = rows if reach else ny
        flux = {i: ext[COND, i] * values[i] for i in values}
        values = {
            i: values[i][:keep] + weight[i, pl.ds(0, keep)] * defect(ITERATE, i, values, flux, keep)
            for i in range(first - reach, last + reach)
        }
    for i in range(nx):
        out_ref[i] = values[first + i][:ny]

    for kind in range(3):
        finish(kind)
    for which, (dx, dy) in enumerate(STEPS):
        @pl.when(exists(dx, dy))
        def _():
            remote_corr(which).wait_send()

    for kind in range(2):
        for off in range(1, n_gy):
            gather(kind, off).wait_send()


def on_device(source, region, permeability, owners, *, n_gx, n_gy):
    nx, ny, nz = source.shape
    planes = nx + 2 * WIDE
    f32 = jnp.float32
    return pl.pallas_call(
        functools.partial(kernel, n_gx, n_gy),
        out_shape=jax.ShapeDtypeStruct(source.shape, f32),
        in_specs=[
            pl.BlockSpec(memory_space=pltpu.HBM),
            pl.BlockSpec(memory_space=pltpu.HBM),
            pl.BlockSpec(memory_space=pltpu.HBM),
            pl.BlockSpec(memory_space=pltpu.HBM),
        ],
        out_specs=pl.BlockSpec(memory_space=pltpu.VMEM),
        scratch_shapes=[
            pltpu.SMEM((1, n_gy), jnp.int32),
            pltpu.VMEM((1, permeability.shape[0]), f32),
            pltpu.VMEM((3, planes, ny + 8, nz), f32),
            pltpu.VMEM((3, 2, nx // 2, 8, nz), f32),
            pltpu.VMEM((3, nx // 2 + 4, 8, nz), f32),
            pltpu.VMEM((3, nx // 2 + 4, 8, nz), f32),
            pltpu.VMEM((nx, ny, nz), jnp.int32),
            pltpu.VMEM((planes, ny + 8, nz), f32),
            pltpu.VMEM((planes, ny + 8, nz), f32),
            pltpu.VMEM((2, nx // 2, n_gy * ny // 2, nz // 2), f32),
            pltpu.VMEM((nx // 2, ny, nz // 2), f32),
            pltpu.VMEM((nx // 2, n_gy * ny // 2, nz // 2), f32),
            pltpu.VMEM((nx // 2 + 2, ny, nz // 2), f32),
            pltpu.VMEM((nx // 2 + 2, ny // 2, nz // 2), f32),
            pltpu.VMEM((2, nx // 2 + 2, 8, nz // 2), f32),
            pltpu.VMEM((nx // 2 + 2, ny + 8, nz), f32),
            pltpu.SemaphoreType.DMA((3, 8)),
            pltpu.SemaphoreType.DMA((3, 8)),
            pltpu.SemaphoreType.DMA((2, n_gy - 1)),
            pltpu.SemaphoreType.DMA((2, n_gy - 1)),
            pltpu.SemaphoreType.DMA((4,)),
            pltpu.SemaphoreType.DMA((8,)),
            pltpu.SemaphoreType.DMA((8,)),
        ],
        compiler_params=pltpu.CompilerParams(
            collective_id=0, has_side_effects=True, vmem_limit_bytes=56328192
        ),
    )(owners, permeability[None, :], source, region)


def solution(mesh):
    placed = (P("gx", "gy", None), P("gx", "gy", None), P(), P("gx", None))
    body = functools.partial(on_device, n_gx=mesh.shape["gx"], n_gy=mesh.shape["gy"])
    return jax.shard_map(
        body, mesh=mesh, in_specs=placed, out_specs=P("gx", "gy", None), check_vma=False
    )
```
